512 devices in a mesh: dom: 128 (over z, y, core), feat: 4 (over x).
Axes of the slice: x: 4, y: 4, z: 16, core: 2. Of those that a mesh axis runs over, the one named last changes fastest.
Arguments:
- features: bfloat16 [32768, 512], P('dom', 'feat'), may hold values from -6 to 6
- w_self: bfloat16 [512, 512], P('feat'), may hold values from -0.25 to 0.25
- w_neigh: bfloat16 [512, 512], P('feat'), may hold values from -0.25 to 0.25
- bias: bfloat16 [512], P('feat'), may hold values from -3 to 3
- cotangent: bfloat16 [32768, 512], P('dom', 'feat'), may hold values from -6 to 6
- tile_vals: bfloat16 [128, 4, 128, 128], P('dom'), may hold values from -0.375 to 0.375
- tile_pos: int32 [128, 4], P('dom'), may hold values from 0 to 3, as said below
- tile_count: int32 [128], P('dom'), may hold values from 1 to 4, as said below
- send_rows: int32 [128, 128, 3], P('dom'), may hold values from 0 to 255
- recv_dest: int32 [128, 128, 3], P('dom'), may hold values from 0 to 255
- ghost_weight: float32 [128, 128, 3], P('dom'), may hold values from 0.2 to 1.8
- recv_count: int32 [128, 128], P('dom'), may hold values from 0 to 3, as said below
- hub_rows: int32 [128, 2], P('dom'), may hold values from 0 to 255, as said below
- hub_weight: bfloat16 [32768, 256], P('dom'), may hold values from -0.375 to 0.375
Outputs:
- output: bfloat16 [32768, 512], P('dom', 'feat')
- grad_features: bfloat16 [32768, 512], P('dom', 'feat')
- grad_self: float32 [512, 512], P('feat')
- grad_neigh: float32 [512, 512], P('feat')
- grad_bias: float32 [512], P('feat')
The draws below stay inside these ranges and needn't reach their ends.
Inputs may be any that keep to these rules, and one draw needn't show every extreme that they name: `tile_pos`: within a partition the numbers are distinct. `tile_count`: some partition uses all 4 slots. `recv_count`: some partition receives 3 live slots from some peer. `hub_rows`: within a partition the rows are distinct.
All inputs are finite; a program needn't handle non-finite values.
Results may differ from the reference program's by a relative error of at most 0.017.
Values may be sent and summed in bfloat16 or wider, within the bound.
A program may use at most 64 MiB of HBM per device.

```python
import math
import jax
import jax.numpy as jnp
from jax import lax

D = 512
TILE = 128
ROWS = 256
HUB_DEV = 2
DOMAINS = 128
NODES = 32768
BLOCKS = 2
TMAX = 4
SLOTS = 3
HUBS = 256


def draw_tile_pos(key, part):
    key = jax.random.fold_in(key, 11)
    keys = jax.random.split(key, DOMAINS)

    def one_domain(domain_key):
        return jax.random.permutation(domain_key, BLOCKS * BLOCKS)[:TMAX].astype(jnp.int32)
    return jax.vmap(one_domain)(keys)


def draw_tile_count(key, part):
    key = jax.random.fold_in(key, 12)
    key_counts, key_busy = jax.random.split(key)
    counts = jax.random.randint(key_counts, (DOMAINS,), TMAX // 4, TMAX // 2 + 1, dtype=jnp.int32)
    busiest = jax.random.randint(key_busy, (), 0, DOMAINS, dtype=jnp.int32)
    return counts.at[busiest].set(TMAX)


def draw_recv_count(key, part):
    key = jax.random.fold_in(key, 13)
    key_counts, key_busy = jax.random.split(key)
    counts = jax.random.randint(key_counts, (DOMAINS, DOMAINS), 0, SLOTS + 1, dtype=jnp.int32)
    busiest = jax.random.randint(key_busy, (2,), 0, DOMAINS, dtype=jnp.int32)
    return counts.at[busiest[0], busiest[1]].set(SLOTS)


def draw_hub_rows(key, part):
    key = jax.random.fold_in(key, 14)
    key_rows, key_pick = jax.random.split(key)
    keys = jax.random.split(key_rows, DOMAINS)
    top_domain = jax.random.randint(key_pick, (), 0, DOMAINS, dtype=jnp.int32)
    low_domain = (top_domain + 1) % DOMAINS

    def one_domain(domain_key, domain_index):
        drawn = jax.random.permutation(domain_key, ROWS)[:HUB_DEV].astype(jnp.int32)
        others = jax.random.permutation(domain_key, ROWS - 1)[:HUB_DEV - 1].astype(jnp.int32)
        with_top = jnp.concatenate([jnp.full((1,), ROWS - 1, jnp.int32), others])
        with_low = jnp.concatenate([jnp.zeros((1,), jnp.int32), others + 1])
        chosen = jnp.where(domain_index == top_domain, with_top, drawn)
        return jnp.where(domain_index == low_domain, with_low, chosen)
    return jax.vmap(one_domain)(keys, jnp.arange(DOMAINS, dtype=jnp.int32))


def with_ends(entries, key, low, high):
    extent = entries.shape
    spot = [jax.random.randint(jax.random.fold_in(key, axis), (), 0, extent[axis]) for axis in range(len(extent))]
    entries = entries.at[tuple(spot)].set(low)
    longest = extent.index(max(extent))
    spot[longest] = (spot[longest] + 1) % extent[longest]
    return entries.at[tuple(spot)].set(high)


def block_scale(key, dims, shards, smallest, largest):
    loudness = 1.0
    for axis_at, shards_of in shards:
        draws = jax.random.uniform(jax.random.fold_in(jax.random.fold_in(key, 6), axis_at), (shards_of,), jnp.float32, smallest / len(shards), largest / len(shards))
        loudness = loudness * jnp.repeat(jnp.exp(draws), dims[axis_at] // shards_of).reshape((-1,) + (1,) * (len(dims) - 1 - axis_at))
    return loudness


def normal_values(stream_key, shape, width, reach, cuts=(), kind=jnp.bfloat16):
    array = width * jax.random.normal(stream_key, shape, jnp.float32)
    if cuts:
        array = array * block_scale(stream_key, shape, cuts, -0.22, 0.18)
    return jnp.clip(array, -reach, reach).astype(kind)


def setup_inputs(seed: int = 0) -> dict:
    arg_keys = jax.random.split(jax.random.key(seed), 15)
    features = normal_values(arg_keys[0], (NODES, D), 1.0, 6.0, ((0, 128), (1, 4)))
    w_self = normal_values(arg_keys[1], (D, D), D ** -0.5, 0.25, ((0, 4),))
    w_neigh = normal_values(arg_keys[2], (D, D), D ** -0.5, 0.25, ((0, 4),))
    bias = normal_values(arg_keys[3], (D,), 0.5, 3.0, ((0, 4),))
    cotangent = normal_values(arg_keys[4], (NODES, D), 1.0, 6.0, ((0, 128), (1, 4)))
    tile_vals = normal_values(arg_keys[5], (DOMAINS, TMAX, TILE, TILE), (2 * TILE) ** -0.5, 0.375, ((0, 128),))
    tile_pos = draw_tile_pos(jax.random.fold_in(arg_keys[14], 71), 0)
    tile_count = draw_tile_count(jax.random.fold_in(arg_keys[14], 71), 0)
    send_rows = with_ends(jax.random.randint(arg_keys[8], (DOMAINS, DOMAINS, SLOTS), 0, ROWS), jax.random.fold_in(arg_keys[8], 1), 0, ROWS - 1).astype(jnp.int32)
    recv_dest = with_ends(jax.random.randint(arg_keys[9], (DOMAINS, DOMAINS, SLOTS), 0, ROWS), jax.random.fold_in(arg_keys[9], 1), 0, ROWS - 1).astype(jnp.int32)
    ghost_weight = jnp.clip(0.2 + 1.5999999 * jax.random.uniform(arg_keys[10], (DOMAINS, DOMAINS, SLOTS), jnp.float32) ** block_scale(arg_keys[10], (DOMAINS, DOMAINS, SLOTS), ((0, 128),), -0.2, 0.2), 0.2, 1.8)
    recv_count = draw_recv_count(jax.random.fold_in(arg_keys[14], 71), 0)
    hub_rows = draw_hub_rows(jax.random.fold_in(arg_keys[14], 71), 0)
    hub_weight = normal_values(arg_keys[13], (NODES, HUBS), HUBS ** -0.5, 0.375, ((0, 128),))
    return {"features": features, "w_self": w_self, "w_neigh": w_neigh, "bias": bias, "cotangent": cotangent, "tile_vals": tile_vals, "tile_pos": tile_pos, "tile_count": tile_count, "send_rows": send_rows, "recv_dest": recv_dest, "ghost_weight": ghost_weight, "recv_count": recv_count, "hub_rows": hub_rows, "hub_weight": hub_weight}


def ghost_coef(ghost_weight, recv_count):
    live = jnp.arange(SLOTS, dtype=jnp.int32)[None, None, :] < recv_count[:, :, None]
    return jnp.where(live, ghost_weight, jnp.zeros_like(ghost_weight))

def local_forward(tile_vals, tile_pos, tile_count, features):

    def per_domain(packed):
        tiles_here, places, count_here, rows_here = packed
        blocks = rows_here.reshape(BLOCKS, TILE, D).astype(jnp.float32)
        taken = blocks[places % BLOCKS]
        used = (jnp.arange(TMAX, dtype=jnp.int32) < count_here).astype(jnp.float32)
        product = jnp.einsum('tij,tjd->tid', tiles_here.astype(jnp.float32), taken) * used[:, None, None]
        summed = jax.ops.segment_sum(product, places // BLOCKS, num_segments=BLOCKS)
        return summed.reshape(ROWS, D)
    packed_all = (tile_vals, tile_pos, tile_count, features.reshape(DOMAINS, ROWS, D))
    return lax.map(per_domain, packed_all).reshape(NODES, D)

def local_backward(tile_vals, tile_pos, tile_count, neigh_grad):

    def per_domain(packed):
        tiles_here, places, count_here, rows_here = packed
        blocks = rows_here.reshape(BLOCKS, TILE, D).astype(jnp.float32)
        taken = blocks[places // BLOCKS]
        used = (jnp.arange(TMAX, dtype=jnp.int32) < count_here).astype(jnp.float32)
        product = jnp.einsum('tij,tid->tjd', tiles_here.astype(jnp.float32), taken) * used[:, None, None]
        summed = jax.ops.segment_sum(product, places % BLOCKS, num_segments=BLOCKS)
        return summed.reshape(ROWS, D)
    packed_all = (tile_vals, tile_pos, tile_count, neigh_grad.reshape(DOMAINS, ROWS, D))
    return lax.map(per_domain, packed_all).reshape(NODES, D)

def ghost_forward(features, send_rows, recv_dest, coef):
    senders = jnp.transpose(send_rows, (1, 0, 2))
    offsets = (jnp.arange(DOMAINS, dtype=jnp.int32) * ROWS)[:, None]

    def per_domain(packed):
        from_rows, dest_here, coef_here = packed
        pulled = features[(offsets + from_rows).astype(jnp.int32)].astype(jnp.float32)
        weighted = pulled * coef_here[:, :, None]
        return jax.ops.segment_sum(weighted.reshape(-1, D), dest_here.reshape(-1), num_segments=ROWS)
    return lax.map(per_domain, (senders, recv_dest, coef)).reshape(NODES, D)

def ghost_backward(neigh_grad, send_rows, recv_dest, coef):
    senders = jnp.transpose(send_rows, (1, 0, 2))
    offsets = (jnp.arange(DOMAINS, dtype=jnp.int32) * ROWS)[:, None]

    def step_domain(totals, packed):
        from_rows, dest_here, coef_here, grad_here = packed
        values = grad_here[dest_here].astype(jnp.float32) * coef_here[:, :, None]
        targets = (offsets + from_rows).astype(jnp.int32).reshape(-1)
        return (totals.at[targets].add(values.reshape(-1, D)), None)
    packed_all = (senders, recv_dest, coef, neigh_grad.reshape(DOMAINS, ROWS, D))
    totals, _ = lax.scan(step_domain, jnp.zeros((NODES, D), jnp.float32), packed_all)
    return totals

def reference(features, w_self, w_neigh, bias, cotangent, tile_vals, tile_pos, tile_count, send_rows, recv_dest, ghost_weight, recv_count, hub_rows, hub_weight):
    coef = ghost_coef(ghost_weight, recv_count)
    local_part = local_forward(tile_vals, tile_pos, tile_count, features)
    ghost_part = ghost_forward(features, send_rows, recv_dest, coef)
    hub_ids = (jnp.arange(DOMAINS, dtype=jnp.int32)[:, None] * ROWS + hub_rows).astype(jnp.int32).reshape(-1)
    hub_part = jnp.dot(hub_weight, features[hub_ids], preferred_element_type=jnp.float32)
    neigh = (local_part + ghost_part + hub_part).astype(jnp.bfloat16)
    preact = jnp.dot(features, w_self, preferred_element_type=jnp.float32) + jnp.dot(neigh, w_neigh, preferred_element_type=jnp.float32) + bias.astype(jnp.float32)
    output = jax.nn.silu(preact).astype(jnp.bfloat16)
    logistic = jax.nn.sigmoid(preact)
    grad_pre = (cotangent.astype(jnp.float32) * logistic * (1.0 + preact * (1.0 - logistic))).astype(jnp.bfloat16)
    neigh_grad = jnp.dot(grad_pre, w_neigh.T, preferred_element_type=jnp.float32).astype(jnp.bfloat16)
    hub_grad = jnp.dot(hub_weight.T, neigh_grad, preferred_element_type=jnp.float32)
    hub_back = jnp.zeros((NODES, D), jnp.float32).at[hub_ids].add(hub_grad)
    grad_total = jnp.dot(grad_pre, w_self.T, preferred_element_type=jnp.float32)
    grad_total = grad_total + local_backward(tile_vals, tile_pos, tile_count, neigh_grad)
    grad_total = grad_total + ghost_backward(neigh_grad, send_rows, recv_dest, coef) + hub_back
    grad_features = grad_total.astype(jnp.bfloat16)
    scale = 1.0 / math.sqrt(NODES)
    grad_self = jnp.dot(features.T, grad_pre, preferred_element_type=jnp.float32) * scale
    grad_neigh = jnp.dot(neigh.T, grad_pre, preferred_element_type=jnp.float32) * scale
    grad_bias = lax.optimization_barrier(jnp.sum(grad_pre.astype(jnp.float32), axis=0)) * scale
    return (output, grad_features, grad_self, grad_neigh, grad_bias)
```

```python
import math

import jax
import jax.numpy as jnp
from jax import lax
from jax.experimental import pallas as pl
from jax.experimental.pallas import tpu as pltpu
from jax.sharding import PartitionSpec as P

Z, Y, CORES, X = 16, 4, 2, 4
YC = Y * CORES
DOM = Z * YC
ROWS, W, TILE = 256, 128, 128
SLOTS, HUB, TMAX = 3, 2, 4
F32, BF16, I32 = jnp.float32, jnp.bfloat16, jnp.int32

ZROWS = 32
B_ROWS = SLOTS * Z + HUB * Z
C_ROWS = B_ROWS + 16

ST_A, ST_B, ST_P, ST_G, ST_C, ST_D, ST_RC, ST_RY, ST_RZ, ST_GZ, ST_GY, ST_GC = range(12)


def iota(shape, axis):
    return lax.broadcasted_iota(I32, shape, axis)


def dot(a, b):
    return jnp.dot(a, b, preferred_element_type=F32)


def dot_t(a, b):
    return lax.dot_general(a, b, (((1,), (1,)), ((), ())), preferred_element_type=F32)


def tdot(a, b):
    return lax.dot_general(a, b, (((0,), (0,)), ((), ())), preferred_element_type=F32)


def onehot(mask):
    return jnp.where(mask, 1.0, 0.0).astype(BF16)


def natural_to_plane():
    n, p = iota((DOM, DOM), 0), iota((DOM, DOM), 1)
    return onehot((n % YC == p // Z) & (n // YC == p % Z))


def hubs_to_plane():
    n, p = iota((DOM * HUB, DOM * HUB), 0), iota((DOM * HUB, DOM * HUB), 1)
    n2, p2 = n // HUB, p // HUB
    return onehot((n % HUB == p % HUB) & (n2 % YC == p2 // Z) & (n2 // YC == p2 % Z))


def hub_pick():
    q, n = iota((HUB * Z, 8 * Z), 0), iota((HUB * Z, 8 * Z), 1)
    return onehot((n // 8 == q // HUB) & (n % 8 == q % HUB))


def kernel(
    feat_h, wself_h, wneigh_h, bias_v, cot_h, tiles_h, pos_s, cnt_s, send_v, dest_v, gw_v, rc_v, hub_s, hw_h,
    out_h, gf_h, gs_h, gn_h, gb_h,
    feat, wself, wneigh, cot, tiles, hw,
    send_a, recv_a, send_b, recv_b, send_p, recv_p, gp, send_c, recv_c, send_d, recv_d,
    g_m, m_m, mt_m, base, pself, wg, rcore, ry, ysum, rz, wtot, out_v, gf_v, gb_v,
    in_sem, out_sem, send_sem, recv_sem,
):
    d = lax.axis_index("dom")
    f = lax.axis_index("feat")
    z, yc = d // YC, d % YC
    y, c = yc // CORES, yc % CORES

    def load(index, src, dst):
        copy = pltpu.make_async_copy(src, dst, in_sem.at[index])
        copy.start()
        return copy

    load_feat = load(0, feat_h, feat)
    load_tiles = load(1, tiles_h, tiles)
    load_hw = load(2, hw_h, hw)
    load_ws = load(3, wself_h, wself)
    load_wn = load(4, wneigh_h, wneigh)
    load_cot = load(5, cot_h, cot)

    def z_peer(k):
        return lax.rem(z + k, Z) * YC + yc

    def plane_peer(k):
        return z * YC + lax.rem(yc + k, YC)

    def y_peer(k):
        return z * YC + lax.rem(y + k, Y) * CORES + c

    partner = z * YC + y * CORES + (1 - c)

    def x_peer(k):
        return lax.rem(f + k, X)

    barrier = pltpu.get_barrier_semaphore()

    def greet(dom, feat_at):
        pl.semaphore_signal(barrier, inc=1, device_id=(dom, feat_at), device_id_type=pl.DeviceIdType.MESH)

    def loop(first, last, step):
        lax.fori_loop(first, last, lambda k, carry: (step(k), carry)[1], 0)

    loop(1, Z, lambda k: greet(z_peer(k), f))
    loop(1, YC, lambda k: greet(plane_peer(k), f))
    loop(1, X, lambda k: greet(d, x_peer(k)))

    def push(stage, src, dst, dom, feat_at):
        pltpu.make_async_remote_copy(
            src_ref=src,
            dst_ref=dst,
            send_sem=send_sem.at[stage],
            recv_sem=recv_sem.at[stage],
            device_id=(dom, feat_at),
            device_id_type=pl.DeviceIdType.MESH,
        ).start()

    def arrived(stage, ref):
        pltpu.make_async_copy(ref, ref, recv_sem.at[stage]).wait()

    def sent(stage, ref):
        pltpu.make_async_copy(ref, ref, send_sem.at[stage]).wait()

    row_of = iota((ROWS, DOM), 0)
    for s in range(SLOTS):
        g_m[:, s * DOM : (s + 1) * DOM] = onehot(row_of == send_v[s])
    lane8, sub8 = iota((8, ROWS), 1), iota((8, ROWS), 0)
    own_hub = onehot(((sub8 == 0) & (lane8 == hub_s[0, 0])) | ((sub8 == 1) & (lane8 == hub_s[0, 1])))
    load_feat.wait()
    groups = [tdot(g_m[:, s * DOM : (s + 1) * DOM], feat[...]).reshape(Z, YC, W) for s in range(SLOTS)]
    groups.append(jnp.broadcast_to(dot(own_hub, feat[...])[None], (Z, 8, W)))
    send_a[...] = jnp.concatenate(groups, axis=1).astype(BF16)

    pl.semaphore_wait(barrier, (Z - 1) + (YC - 1) + (X - 1))
    loop(1, Z, lambda k: push(ST_A, send_a.at[lax.rem(z + k, Z)], recv_a.at[z], z_peer(k), f))
    recv_a[pl.ds(z, 1)] = send_a[pl.ds(z, 1)]

    to_plane = natural_to_plane()
    pick = hub_pick()
    live = [jnp.where(rc_v[...] > s, gw_v[s], 0.0) for s in range(SLOTS)]
    packed = jnp.concatenate([dest_v[s].astype(F32) for s in range(SLOTS)] + live + [jnp.zeros((2, DOM), F32)], axis=0)
    packed = dot(packed.astype(BF16), to_plane)
    for s in range(SLOTS):
        dest_row = packed[s : s + 1].astype(I32)
        m_m[:, ROWS + s * DOM : ROWS + (s + 1) * DOM] = jnp.where(
            row_of == dest_row, packed[SLOTS + s : SLOTS + s + 1], 0.0
        ).astype(BF16)

    arrived(ST_A, recv_a.at[pl.ds(0, Z - 1)])
    got = recv_a[...].astype(F32)
    for s in range(SLOTS):
        part = got[:, s * YC : (s + 1) * YC].reshape(DOM, W).astype(BF16)
        send_b[:, s * Z : (s + 1) * Z] = tdot(to_plane, part).reshape(YC, Z, W).astype(BF16)
    hub_rows = dot(pick, got[:, SLOTS * YC :].reshape(Z * 8, W).astype(BF16))
    send_b[:, SLOTS * Z :] = jnp.broadcast_to(hub_rows[None], (YC, HUB * Z, W)).astype(BF16)
    loop(1, YC, lambda k: push(ST_B, send_b.at[lax.rem(yc + k, YC)], recv_b.at[yc], plane_peer(k), f))
    recv_b[pl.ds(yc, 1)] = send_b[pl.ds(yc, 1)]

    load_tiles.wait()
    tile_f32 = [tiles[0, t].astype(F32) for t in range(TMAX)]
    for k in range(4):
        block = jnp.zeros((TILE, TILE), F32)
        for t in range(TMAX):
            used = jnp.where((pos_s[0, t] == k) & (cnt_s[0] > t), 1.0, 0.0)
            block = block + used * tile_f32[t]
        m_m[(k // 2) * TILE : (k // 2 + 1) * TILE, (k % 2) * TILE : (k % 2 + 1) * TILE] = block.astype(BF16)
    load_hw.wait()
    m_m[:, ROWS + SLOTS * DOM :] = dot(hw[...], hubs_to_plane()).astype(BF16)
    base[...] = dot(m_m[:, :ROWS], feat[...])
    load_ws.wait()
    pself[...] = dot(feat[...], wself[...])
    load_wn.wait()

    arrived(ST_B, recv_b.at[pl.ds(0, YC - 1)])
    pulled = [recv_b[:, s * Z : (s + 1) * Z].reshape(DOM, W) for s in range(SLOTS)]
    pulled.append(recv_b[:, SLOTS * Z :].reshape(DOM * HUB, W))
    neigh = (base[...] + dot(m_m[:, ROWS:], jnp.concatenate(pulled, axis=0))).astype(BF16)
    partial = (pself[...] + dot(neigh, wneigh[...])).astype(BF16)
    for j in range(X):
        send_p[j] = partial[:, j * W : (j + 1) * W]
    loop(1, X, lambda k: push(ST_P, send_p.at[x_peer(k)], recv_p.at[f], d, x_peer(k)))
    recv_p[pl.ds(f, 1)] = send_p[pl.ds(f, 1)]

    mt_m[...] = m_m[...].T
    load_cot.wait()

    arrived(ST_P, recv_p.at[pl.ds(0, X - 1)])
    preact = jnp.sum(recv_p[...].astype(F32), axis=0) + bias_v[...].astype(F32)
    logistic = jax.nn.sigmoid(preact)
    out_v[...] = (preact * logistic).astype(BF16)
    grad_pre = (cot[...].astype(F32) * logistic * (1.0 + preact * (1.0 - logistic))).astype(BF16)
    gp[pl.ds(f, 1)] = grad_pre[None]
    loop(1, X, lambda k: push(ST_G, gp.at[f], gp.at[f], d, x_peer(k)))
    save_out = pltpu.make_async_copy(out_v, out_h, out_sem.at[0])
    save_out.start()
    bias_part = jnp.sum(grad_pre.astype(F32), axis=0, keepdims=True)

    arrived(ST_G, gp.at[pl.ds(0, X - 1)])
    gp_full = jnp.concatenate([gp[j] for j in range(X)], axis=1)
    neigh_grad = dot_t(gp_full, wneigh[...]).astype(BF16)
    back = dot(mt_m[...], neigh_grad)
    for s in range(SLOTS):
        at = ROWS + s * DOM
        send_c[:, s * Z : (s + 1) * Z] = back[at : at + DOM].reshape(YC, Z, W).astype(BF16)
    send_c[:, SLOTS * Z : B_ROWS] = back[ROWS + SLOTS * DOM :].reshape(YC, HUB * Z, W).astype(BF16)
    base[...] = back[:ROWS]

    def two_rows(row, first):
        high = row.astype(BF16).astype(F32)
        at = iota((8, W), 0)
        return jnp.where(at == first, high, jnp.where(at == first + 1, row - high, 0.0))

    bias_rows = jnp.concatenate([two_rows(bias_part, 0), jnp.zeros((8, W), F32)], axis=0)
    send_c[:, B_ROWS:] = jnp.broadcast_to(bias_rows[None], (YC, 16, W)).astype(BF16)
    loop(1, YC, lambda k: push(ST_C, send_c.at[lax.rem(yc + k, YC)], recv_c.at[yc], plane_peer(k), f))
    recv_c[pl.ds(yc, 1)] = send_c[pl.ds(yc, 1)]

    wg[0] = jnp.stack([tdot(feat[...], gp[j]) for j in range(X)])
    wg[1] = jnp.stack([tdot(neigh, gp[j]) for j in range(X)])
    push(ST_RC, wg.at[1 - c], rcore, partner, f)
    base[...] = base[...] + dot_t(gp_full, wself[...])

    arrived(ST_C, recv_c.at[pl.ds(0, YC - 1)])
    groups = []
    for s in range(SLOTS):
        part = recv_c[:, s * Z : (s + 1) * Z].reshape(DOM, W)
        groups.append(dot(to_plane, part).reshape(Z, YC, W))
    hub_sum = jnp.sum(recv_c[:, SLOTS * Z : B_ROWS].astype(F32), axis=0)
    bias_sum = jnp.sum(recv_c[:, B_ROWS:].astype(F32), axis=0)
    bias_sum = bias_sum[0:1] + bias_sum[1:2]
    tail = tdot(pick, hub_sum.astype(BF16)).reshape(Z, 8, W) + two_rows(bias_sum, HUB)[None]
    groups.append(tail)
    send_d[...] = jnp.concatenate(groups, axis=1).astype(BF16)
    loop(1, Z, lambda k: push(ST_D, send_d.at[lax.rem(z + k, Z)], recv_d.at[z], z_peer(k), f))
    recv_d[pl.ds(z, 1)] = send_d[pl.ds(z, 1)]

    arrived(ST_RC, rcore)
    rcore[...] = rcore[...] + wg[pl.ds(c, 1)].reshape(Y, W, W)
    loop(1, Y, lambda k: push(ST_RY, rcore.at[lax.rem(y + k, Y)], ry.at[y], y_peer(k), f))
    ry[pl.ds(y, 1)] = rcore[pl.ds(y, 1)]
    arrived(ST_RY, ry.at[pl.ds(0, Y - 1)])
    over_y = ry[0] + ry[1] + ry[2] + ry[3]
    ysum[...] = over_y

    loop(
        1,
        Z,
        lambda k: push(
            ST_RZ,
            ysum.at[pl.ds(pl.multiple_of(lax.rem(z + k, Z) * 8, 8), 8)],
            rz.at[z],
            z_peer(k),
            f,
        ),
    )
    mine = pl.ds(pl.multiple_of(z * 8, 8), 8)
    rz[pl.ds(z, 1)] = ysum[mine][None]

    arrived(ST_D, recv_d.at[pl.ds(0, Z - 1)])
    got = recv_d[...].astype(F32)
    pieces = [got[:, s * YC : (s + 1) * YC].reshape(DOM, W).astype(BF16) for s in range(SLOTS)]
    total = base[...] + dot(g_m[...], jnp.concatenate(pieces, axis=0))
    last = jnp.sum(got[:, SLOTS * YC :], axis=0)
    at_row = iota((ROWS, W), 0)
    for k in range(HUB):
        total = total + jnp.where(at_row == hub_s[0, k], last[k : k + 1], 0.0)
    gf_v[...] = total.astype(BF16)
    scale = 1.0 / math.sqrt(DOM * ROWS)
    gb_v[...] = (last[HUB : HUB + 1] + last[HUB + 1 : HUB + 2]) * scale
    save_gf = pltpu.make_async_copy(gf_v, gf_h, out_sem.at[1])
    save_gf.start()
    save_gb = pltpu.make_async_copy(gb_v, gb_h, out_sem.at[2])
    save_gb.start()

    arrived(ST_RZ, rz.at[pl.ds(0, Z - 1)])
    wtot[c, y, mine] = jnp.sum(rz[...], axis=0) * scale
    loop(1, Z, lambda k: push(ST_GZ, wtot.at[c, y, mine], wtot.at[c, y, mine], z_peer(k), f))
    arrived(ST_GZ, wtot.at[c, y, pl.ds(0, (Z - 1) * 8)])
    loop(1, Y, lambda k: push(ST_GY, wtot.at[c, y], wtot.at[c, y], y_peer(k), f))
    arrived(ST_GY, wtot.at[c, pl.ds(0, Y - 1)])
    push(ST_GC, wtot.at[c], wtot.at[c], partner, f)
    arrived(ST_GC, wtot.at[1 - c])
    saves = [save_out, save_gf, save_gb]
    for i, target in enumerate((gs_h, gn_h)):
        for j in range(X):
            copy = pltpu.make_async_copy(wtot.at[i, j], target.at[:, pl.ds(j * W, W)], out_sem.at[3 + i * X + j])
            copy.start()
            saves.append(copy)

    sent(ST_A, send_a.at[pl.ds(0, Z - 1)])
    sent(ST_B, send_b.at[pl.ds(0, YC - 1)])
    sent(ST_P, send_p.at[pl.ds(0, X - 1)])
    sent(ST_G, gp.at[pl.ds(0, X - 1)])
    sent(ST_C, send_c.at[pl.ds(0, YC - 1)])
    sent(ST_D, send_d.at[pl.ds(0, Z - 1)])
    sent(ST_RC, rcore)
    sent(ST_RY, ry.at[pl.ds(0, Y - 1)])
    sent(ST_RZ, rz.at[pl.ds(0, Z - 1)])
    sent(ST_GZ, rz.at[pl.ds(0, Z - 1)])
    sent(ST_GY, ry.at[pl.ds(0, Y - 1)])
    sent(ST_GC, rcore)
    for copy in saves:
        copy.wait()


def on_device(
    features, w_self, w_neigh, bias, cotangent, tile_vals, tile_pos, tile_count,
    send_rows, recv_dest, ghost_weight, recv_count, hub_rows, hub_weight,
):
    def by_slot(array):
        return jnp.transpose(array, (2, 0, 1))

    hbm = pl.BlockSpec(memory_space=pl.ANY)
    vmem = pl.BlockSpec(memory_space=pltpu.VMEM)
    smem = pl.BlockSpec(memory_space=pltpu.SMEM)
    cols = X * W
    rest = SLOTS * DOM + HUB * DOM
    output, grad_features, grad_self, grad_neigh, grad_bias = pl.pallas_call(
        kernel,
        out_shape=(
            jax.ShapeDtypeStruct((ROWS, W), BF16),
            jax.ShapeDtypeStruct((ROWS, W), BF16),
            jax.ShapeDtypeStruct((W, cols), F32),
            jax.ShapeDtypeStruct((W, cols), F32),
            jax.ShapeDtypeStruct((1, W), F32),
        ),
        in_specs=[hbm, hbm, hbm, vmem, hbm, hbm, smem, smem, vmem, vmem, vmem, vmem, smem, hbm],
        out_specs=(hbm,) * 5,
        scratch_shapes=[
            pltpu.VMEM((ROWS, W), BF16),
            pltpu.VMEM((W, cols), BF16),
            pltpu.VMEM((W, cols), BF16),
            pltpu.VMEM((ROWS, W), BF16),
            pltpu.VMEM((1, TMAX, TILE, TILE), BF16),
            pltpu.VMEM((ROWS, HUB * DOM), BF16),
            pltpu.VMEM((Z, ZROWS, W), BF16),
            pltpu.VMEM((Z, ZROWS, W), BF16),
            pltpu.VMEM((YC, B_ROWS, W), BF16),
            pltpu.VMEM((YC, B_ROWS, W), BF16),
            pltpu.VMEM((X, ROWS, W), BF16),
            pltpu.VMEM((X, ROWS, W), BF16),
            pltpu.VMEM((X, ROWS, W), BF16),
            pltpu.VMEM((YC, C_ROWS, W), BF16),
            pltpu.VMEM((YC, C_ROWS, W), BF16),
            pltpu.VMEM((Z, ZROWS, W), BF16),
            pltpu.VMEM((Z, ZROWS, W), BF16),
            pltpu.VMEM((ROWS, SLOTS * DOM), BF16),
            pltpu.VMEM((ROWS, ROWS + rest), BF16),
            pltpu.VMEM((ROWS + rest, ROWS), BF16),
            pltpu.VMEM((ROWS, W), F32),
            pltpu.VMEM((ROWS, cols), F32),
            pltpu.VMEM((2, Y, W, W), F32),
            pltpu.VMEM((Y, W, W), F32),
            pltpu.VMEM((Y, W, W), F32),
            pltpu.VMEM((W, W), F32),
            pltpu.VMEM((Z, 8, W), F32),
            pltpu.VMEM((2, Y, W, W), F32),
            pltpu.VMEM((ROWS, W), BF16),
            pltpu.VMEM((ROWS, W), BF16),
            pltpu.VMEM((1, W), F32),
            pltpu.SemaphoreType.DMA((6,)),
            pltpu.SemaphoreType.DMA((11,)),
            pltpu.SemaphoreType.DMA((12,)),
            pltpu.SemaphoreType.DMA((12,)),
        ],
        compiler_params=pltpu.CompilerParams(
            collective_id=0, has_side_effects=True, vmem_limit_bytes=32 * 1024 * 1024
        ),
    )(
        features, w_self, w_neigh, bias.reshape(1, W), cotangent, tile_vals, tile_pos, tile_count,
        by_slot(send_rows), by_slot(recv_dest), by_slot(ghost_weight), recv_count, hub_rows, hub_weight,
    )
    return output, grad_features, grad_self, grad_neigh, grad_bias.reshape(W)


def solution(mesh):
    placed = (
        P("dom", "feat"),
        P("feat", None),
        P("feat", None),
        P("feat"),
        P("dom", "feat"),
        P("dom", None, None, None),
        P("dom", None),
        P("dom"),
        P("dom", None, None),
        P("dom", None, None),
        P("dom", None, None),
        P("dom", None),
        P("dom", None),
        P("dom", None),
    )
    return jax.shard_map(
        on_device,
        mesh=mesh,
        in_specs=placed,
        out_specs=(P("dom", "feat"), P("dom", "feat"), P("feat", None), P("feat", None), P("feat")),
        check_vma=False,
    )
```

```python
import math

import jax
import jax.numpy as jnp
from jax import lax
from jax.experimental import pallas as pl
from jax.experimental.pallas import tpu as pltpu
from jax.sharding import PartitionSpec as P

Z, Y, CORES, X = 16, 4, 2, 4
YC = Y * CORES
DOM = Z * YC
ROWS, W, TILE = 256, 128, 128
SLOTS, HUB, TMAX = 3, 2, 4
F32, BF16, I32 = jnp.float32, jnp.bfloat16, jnp.int32

ZROWS = 32
B_ROWS = SLOTS * Z + HUB * Z
C_ROWS = B_ROWS + 16

ST_A, ST_B, ST_P, ST_G, ST_C, ST_D, ST_RC, ST_RY, ST_RZ, ST_GZ, ST_GY, ST_GC = range(12)


def iota(shape, axis):
    return lax.broadcasted_iota(I32, shape, axis)


def dot(a, b):
    return jnp.dot(a, b, preferred_element_type=F32)


def dot_t(a, b):
    return lax.dot_general(a, b, (((1,), (1,)), ((), ())), preferred_element_type=F32)


def tdot(a, b):
    return lax.dot_general(a, b, (((0,), (0,)), ((), ())), preferred_element_type=F32)


def onehot(mask):
    return jnp.where(mask, 1.0, 0.0).astype(BF16)


def natural_to_plane():
    n, p = iota((DOM, DOM), 0), iota((DOM, DOM), 1)
    return onehot((n % YC == p // Z) & (n // YC == p % Z))


def hubs_to_plane():
    n, p = iota((DOM * HUB, DOM * HUB), 0), iota((DOM * HUB, DOM * HUB), 1)
    n2, p2 = n // HUB, p // HUB
    return onehot((n % HUB == p % HUB) & (n2 % YC == p2 // Z) & (n2 // YC == p2 % Z))


def hub_pick():
    q, n = iota((HUB * Z, 8 * Z), 0), iota((HUB * Z, 8 * Z), 1)
    return onehot((n // 8 == q // HUB) & (n % 8 == q % HUB))


def kernel(
    feat_h, wself_h, wneigh_h, bias_h, cot_h, tiles_h, pos_h, cnt_s, send_h, dest_h, gw_h, rc_h, hub_h, hw_h,
    out_v, gf_v, wtot, gb_v,
    feat, wself, wneigh, bias_v, cot, tiles, pos_s, send_v, dest_v, gw_v, rc_v, hub_s, hw,
    send_a, recv_a, send_b, recv_b, send_p, recv_p, gp, send_c, recv_c, send_d, recv_d,
    g_m, m_m, mt_m, base, pself, wg, rcore, ry, ysum, rz,
    in_sem, send_sem, recv_sem,
):
    d = lax.axis_index("dom")
    f = lax.axis_index("feat")
    z, yc = d // YC, d % YC
    y, c = yc // CORES, yc % CORES

    loads = []

    def load(src, dst):
        copy = pltpu.make_async_copy(src, dst, in_sem.at[len(loads)])
        copy.start()
        loads.append(copy)
        return copy

    load_send = load(send_h, send_v)
    load_hub = load(hub_h, hub_s)
    load_feat = load(feat_h, feat)
    load_edges = [load(dest_h, dest_v), load(gw_h, gw_v), load(rc_h, rc_v)]
    load_tiles = [load(tiles_h, tiles), load(pos_h, pos_s)]
    load_hw = load(hw_h, hw)
    load_ws = load(wself_h, wself)
    load_wn = load(wneigh_h, wneigh)
    load_cot = [load(cot_h, cot), load(bias_h, bias_v)]

    def z_peer(k):
        return lax.rem(z + k, Z) * YC + yc

    def plane_peer(k):
        return z * YC + lax.rem(yc + k, YC)

    def y_peer(k):
        return z * YC + lax.rem(y + k, Y) * CORES + c

    partner = z * YC + y * CORES + (1 - c)

    def x_peer(k):
        return lax.rem(f + k, X)

    barrier = pltpu.get_barrier_semaphore()

    def greet(dom, feat_at):
        pl.semaphore_signal(barrier, inc=1, device_id=(dom, feat_at), device_id_type=pl.DeviceIdType.MESH)

    def loop(first, last, step):
        lax.fori_loop(first, last, lambda k, carry: (step(k), carry)[1], 0)

    loop(1, Z, lambda k: greet(z_peer(k), f))
    loop(1, YC, lambda k: greet(plane_peer(k), f))
    loop(1, X, lambda k: greet(d, x_peer(k)))

    def push(stage, src, dst, dom, feat_at):
        pltpu.make_async_remote_copy(
            src_ref=src,
            dst_ref=dst,
            send_sem=send_sem.at[stage],
            recv_sem=recv_sem.at[stage],
            device_id=(dom, feat_at),
            device_id_type=pl.DeviceIdType.MESH,
        ).start()

    def arrived(stage, ref):
        pltpu.make_async_copy(ref, ref, recv_sem.at[stage]).wait()

    def sent(stage, ref):
        pltpu.make_async_copy(ref, ref, send_sem.at[stage]).wait()

    pending = []

    row_of = iota((ROWS, DOM), 0)
    load_send.wait()
    load_hub.wait()
    for s in range(SLOTS):
        g_m[:, s * DOM : (s + 1) * DOM] = onehot(row_of == send_v[s])
    lane8, sub8 = iota((8, ROWS), 1), iota((8, ROWS), 0)
    own_hub = onehot(((sub8 == 0) & (lane8 == hub_s[0, 0])) | ((sub8 == 1) & (lane8 == hub_s[0, 1])))
    load_feat.wait()
    groups = [tdot(g_m[:, s * DOM : (s + 1) * DOM], feat[...]).reshape(Z, YC, W) for s in range(SLOTS)]
    groups.append(jnp.broadcast_to(dot(own_hub, feat[...])[None], (Z, 8, W)))
    send_a[...] = jnp.concatenate(groups, axis=1).astype(BF16)

    pl.semaphore_wait(barrier, (Z - 1) + (YC - 1) + (X - 1))
    loop(1, Z, lambda k: push(ST_A, send_a.at[lax.rem(z + k, Z)], recv_a.at[z], z_peer(k), f))
    pending.append((ST_A, send_a.at[pl.ds(0, Z - 1)]))
    recv_a[pl.ds(z, 1)] = send_a[pl.ds(z, 1)]

    to_plane = natural_to_plane()
    pick = hub_pick()
    for copy in load_edges:
        copy.wait()
    live = [jnp.where(rc_v[...] > s, gw_v[s], 0.0) for s in range(SLOTS)]
    packed = jnp.concatenate([dest_v[s].astype(F32) for s in range(SLOTS)] + live + [jnp.zeros((2, DOM), F32)], axis=0)
    packed = dot(packed.astype(BF16), to_plane)
    for s in range(SLOTS):
        dest_row = packed[s : s + 1].astype(I32)
        m_m[:, ROWS + s * DOM : ROWS + (s + 1) * DOM] = jnp.where(
            row_of == dest_row, packed[SLOTS + s : SLOTS + s + 1], 0.0
        ).astype(BF16)

    arrived(ST_A, recv_a.at[pl.ds(0, Z - 1)])
    got = recv_a[...].astype(F32)
    for s in range(SLOTS):
        part = got[:, s * YC : (s + 1) * YC].reshape(DOM, W).astype(BF16)
        send_b[:, s * Z : (s + 1) * Z] = tdot(to_plane, part).reshape(YC, Z, W).astype(BF16)
    hub_rows = dot(pick, got[:, SLOTS * YC :].reshape(Z * 8, W).astype(BF16))
    send_b[:, SLOTS * Z :] = jnp.broadcast_to(hub_rows[None], (YC, HUB * Z, W)).astype(BF16)
    loop(1, YC, lambda k: push(ST_B, send_b.at[lax.rem(yc + k, YC)], recv_b.at[yc], plane_peer(k), f))
    pending.append((ST_B, send_b.at[pl.ds(0, YC - 1)]))
    recv_b[pl.ds(yc, 1)] = send_b[pl.ds(yc, 1)]

    for copy in load_tiles:
        copy.wait()
    tile_f32 = [tiles[0, t].astype(F32) for t in range(TMAX)]
    for k in range(4):
        block = jnp.zeros((TILE, TILE), F32)
        for t in range(TMAX):
            used = jnp.where((pos_s[0, t] == k) & (cnt_s[0] > t), 1.0, 0.0)
            block = block + used * tile_f32[t]
        m_m[(k // 2) * TILE : (k // 2 + 1) * TILE, (k % 2) * TILE : (k % 2 + 1) * TILE] = block.astype(BF16)
    load_hw.wait()
    m_m[:, ROWS + SLOTS * DOM :] = dot(hw[...], hubs_to_plane()).astype(BF16)
    base[...] = dot(m_m[:, :ROWS], feat[...])
    load_ws.wait()
    pself[...] = dot(feat[...], wself[...])
    load_wn.wait()

    arrived(ST_B, recv_b.at[pl.ds(0, YC - 1)])
    pulled = [recv_b[:, s * Z : (s + 1) * Z].reshape(DOM, W) for s in range(SLOTS)]
    pulled.append(recv_b[:, SLOTS * Z :].reshape(DOM * HUB, W))
    neigh = (base[...] + dot(m_m[:, ROWS:], jnp.concatenate(pulled, axis=0))).astype(BF16)
    partial = (pself[...] + dot(neigh, wneigh[...])).astype(BF16)
    for j in range(X):
        send_p[j] = partial[:, j * W : (j + 1) * W]
    loop(1, X, lambda k: push(ST_P, send_p.at[x_peer(k)], recv_p.at[f], d, x_peer(k)))
    pending.append((ST_P, send_p.at[pl.ds(0, X - 1)]))
    recv_p[pl.ds(f, 1)] = send_p[pl.ds(f, 1)]

    mt_m[...] = m_m[...].T
    for copy in load_cot:
        copy.wait()

    arrived(ST_P, recv_p.at[pl.ds(0, X - 1)])
    preact = jnp.sum(recv_p[...].astype(F32), axis=0) + bias_v[...].astype(F32)
    logistic = jax.nn.sigmoid(preact)
    out_v[...] = (preact * logistic).astype(BF16)
    grad_pre = (cot[...].astype(F32) * logistic * (1.0 + preact * (1.0 - logistic))).astype(BF16)
    gp[pl.ds(f, 1)] = grad_pre[None]
    loop(1, X, lambda k: push(ST_G, gp.at[f], gp.at[f], d, x_peer(k)))
    pending.append((ST_G, gp.at[pl.ds(0, X - 1)]))
    bias_part = jnp.sum(grad_pre.astype(F32), axis=0, keepdims=True)

    arrived(ST_G, gp.at[pl.ds(0, X - 1)])
    gp_full = jnp.concatenate([gp[j] for j in range(X)], axis=1)
    neigh_grad = dot_t(gp_full, wneigh[...]).astype(BF16)
    back = dot(mt_m[...], neigh_grad)
    for s in range(SLOTS):
        at = ROWS + s * DOM
        send_c[:, s * Z : (s + 1) * Z] = back[at : at + DOM].reshape(YC, Z, W).astype(BF16)
    send_c[:, SLOTS * Z : B_ROWS] = back[ROWS + SLOTS * DOM :].reshape(YC, HUB * Z, W).astype(BF16)
    base[...] = back[:ROWS]

    def two_rows(row, first):
        high = row.astype(BF16).astype(F32)
        at = iota((8, W), 0)
        return jnp.where(at == first, high, jnp.where(at == first + 1, row - high, 0.0))

    bias_rows = jnp.concatenate([two_rows(bias_part, 0), jnp.zeros((8, W), F32)], axis=0)
    send_c[:, B_ROWS:] = jnp.broadcast_to(bias_rows[None], (YC, 16, W)).astype(BF16)
    loop(1, YC, lambda k: push(ST_C, send_c.at[lax.rem(yc + k, YC)], recv_c.at[yc], plane_peer(k), f))
    pending.append((ST_C, send_c.at[pl.ds(0, YC - 1)]))
    recv_c[pl.ds(yc, 1)] = send_c[pl.ds(yc, 1)]

    wg[0] = jnp.stack([tdot(feat[...], gp[j]) for j in range(X)])
    wg[1] = jnp.stack([tdot(neigh, gp[j]) for j in range(X)])
    push(ST_RC, wg.at[1 - c], rcore, partner, f)
    pending.append((ST_RC, rcore))
    base[...] = base[...] + dot_t(gp_full, wself[...])

    arrived(ST_C, recv_c.at[pl.ds(0, YC - 1)])
    groups = []
    for s in range(SLOTS):
        part = recv_c[:, s * Z : (s + 1) * Z].reshape(DOM, W)
        groups.append(dot(to_plane, part).reshape(Z, YC, W))
    hub_sum = jnp.sum(recv_c[:, SLOTS * Z : B_ROWS].astype(F32), axis=0)
    bias_sum = jnp.sum(recv_c[:, B_ROWS:].astype(F32), axis=0)
    bias_sum = bias_sum[0:1] + bias_sum[1:2]
    tail = tdot(pick, hub_sum.astype(BF16)).reshape(Z, 8, W) + two_rows(bias_sum, HUB)[None]
    groups.append(tail)
    send_d[...] = jnp.concatenate(groups, axis=1).astype(BF16)
    loop(1, Z, lambda k: push(ST_D, send_d.at[lax.rem(z + k, Z)], recv_d.at[z], z_peer(k), f))
    pending.append((ST_D, send_d.at[pl.ds(0, Z - 1)]))
    recv_d[pl.ds(z, 1)] = send_d[pl.ds(z, 1)]

    arrived(ST_RC, rcore)
    rcore[...] = rcore[...] + wg[pl.ds(c, 1)].reshape(Y, W, W)
    loop(1, Y, lambda k: push(ST_RY, rcore.at[lax.rem(y + k, Y)], ry.at[y], y_peer(k), f))
    pending.append((ST_RY, ry.at[pl.ds(0, Y - 1)]))
    ry[pl.ds(y, 1)] = rcore[pl.ds(y, 1)]
    arrived(ST_RY, ry.at[pl.ds(0, Y - 1)])
    over_y = ry[0] + ry[1] + ry[2] + ry[3]
    ysum[...] = over_y

    loop(
        1,
        Z,
        lambda k: push(
            ST_RZ,
            ysum.at[pl.ds(pl.multiple_of(lax.rem(z + k, Z) * 8, 8), 8)],
            rz.at[z],
            z_peer(k),
            f,
        ),
    )
    pending.append((ST_RZ, rz.at[pl.ds(0, Z - 1)]))
    mine = pl.ds(pl.multiple_of(z * 8, 8), 8)
    rz[pl.ds(z, 1)] = ysum[mine][None]

    arrived(ST_D, recv_d.at[pl.ds(0, Z - 1)])
    got = recv_d[...].astype(F32)
    pieces = [got[:, s * YC : (s + 1) * YC].reshape(DOM, W).astype(BF16) for s in range(SLOTS)]
    total = base[...] + dot(g_m[...], jnp.concatenate(pieces, axis=0))
    last = jnp.sum(got[:, SLOTS * YC :], axis=0)
    at_row = iota((ROWS, W), 0)
    for k in range(HUB):
        total = total + jnp.where(at_row == hub_s[0, k], last[k : k + 1], 0.0)
    gf_v[...] = total.astype(BF16)
    scale = 1.0 / math.sqrt(DOM * ROWS)
    gb_v[...] = (last[HUB : HUB + 1] + last[HUB + 1 : HUB + 2]) * scale

    arrived(ST_RZ, rz.at[pl.ds(0, Z - 1)])
    wtot[c, y, mine] = jnp.sum(rz[...], axis=0) * scale
    loop(1, Z, lambda k: push(ST_GZ, wtot.at[c, y, mine], wtot.at[c, y, mine], z_peer(k), f))
    pending.append((ST_GZ, rz.at[pl.ds(0, Z - 1)]))
    arrived(ST_GZ, wtot.at[c, y, pl.ds(0, (Z - 1) * 8)])
    loop(1, Y, lambda k: push(ST_GY, wtot.at[c, y], wtot.at[c, y], y_peer(k), f))
    pending.append((ST_GY, ry.at[pl.ds(0, Y - 1)]))
    arrived(ST_GY, wtot.at[c, pl.ds(0, Y - 1)])
    push(ST_GC, wtot.at[c], wtot.at[c], partner, f)
    pending.append((ST_GC, rcore))
    arrived(ST_GC, wtot.at[1 - c])

    for stage, ref in pending:
        sent(stage, ref)


def save_kernel(out_v, gf_v, wtot, gb_v, out_h, gf_h, gs_h, gn_h, gb_h, sem):
    copies = [(out_v, out_h), (gf_v, gf_h), (gb_v, gb_h)]
    for i, target in enumerate((gs_h, gn_h)):
        copies += [(wtot.at[i, j], target.at[:, pl.ds(j * W, W)]) for j in range(X)]
    copies = [pltpu.make_async_copy(src, dst, sem.at[i]) for i, (src, dst) in enumerate(copies)]
    for copy in copies:
        copy.start()
    for copy in copies:
        copy.wait()


def on_device(
    features, w_self, w_neigh, bias, cotangent, tile_vals, tile_pos, tile_count,
    send_rows, recv_dest, ghost_weight, recv_count, hub_rows, hub_weight,
):
    def by_slot(array):
        return jnp.transpose(array, (2, 0, 1))

    hbm = pl.BlockSpec(memory_space=pltpu.HBM)
    vmem = pl.BlockSpec(memory_space=pltpu.VMEM)
    cols = X * W
    rest = SLOTS * DOM + HUB * DOM
    results = pl.pallas_call(
        kernel,
        out_shape=(
            jax.ShapeDtypeStruct((ROWS, W), BF16),
            jax.ShapeDtypeStruct((ROWS, W), BF16),
            jax.ShapeDtypeStruct((2, Y, W, W), F32),
            jax.ShapeDtypeStruct((1, W), F32),
        ),
        in_specs=[hbm] * 7 + [pl.BlockSpec(memory_space=pltpu.SMEM)] + [hbm] * 6,
        out_specs=(vmem,) * 4,
        scratch_shapes=[
            pltpu.VMEM((ROWS, W), BF16),
            pltpu.VMEM((W, cols), BF16),
            pltpu.VMEM((W, cols), BF16),
            pltpu.VMEM((1, W), BF16),
            pltpu.VMEM((ROWS, W), BF16),
            pltpu.VMEM((1, TMAX, TILE, TILE), BF16),
            pltpu.SMEM((1, TMAX), I32),
            pltpu.VMEM((SLOTS, 1, DOM), I32),
            pltpu.VMEM((SLOTS, 1, DOM), I32),
            pltpu.VMEM((SLOTS, 1, DOM), F32),
            pltpu.VMEM((1, DOM), I32),
            pltpu.SMEM((1, HUB), I32),
            pltpu.VMEM((ROWS, HUB * DOM), BF16),
            pltpu.VMEM((Z, ZROWS, W), BF16),
            pltpu.VMEM((Z, ZROWS, W), BF16),
            pltpu.VMEM((YC, B_ROWS, W), BF16),
            pltpu.VMEM((YC, B_ROWS, W), BF16),
            pltpu.VMEM((X, ROWS, W), BF16),
            pltpu.VMEM((X, ROWS, W), BF16),
            pltpu.VMEM((X, ROWS, W), BF16),
            pltpu.VMEM((YC, C_ROWS, W), BF16),
            pltpu.VMEM((YC, C_ROWS, W), BF16),
            pltpu.VMEM((Z, ZROWS, W), BF16),
            pltpu.VMEM((Z, ZROWS, W), BF16),
            pltpu.VMEM((ROWS, SLOTS * DOM), BF16),
            pltpu.VMEM((ROWS, ROWS + rest), BF16),
            pltpu.VMEM((ROWS + rest, ROWS), BF16),
            pltpu.VMEM((ROWS, W), F32),
            pltpu.VMEM((ROWS, cols), F32),
            pltpu.VMEM((2, Y, W, W), F32),
            pltpu.VMEM((Y, W, W), F32),
            pltpu.VMEM((Y, W, W), F32),
            pltpu.VMEM((W, W), F32),
            pltpu.VMEM((Z, 8, W), F32),
            pltpu.SemaphoreType.DMA((13,)),
            pltpu.SemaphoreType.DMA((12,)),
            pltpu.SemaphoreType.DMA((12,)),
        ],
        compiler_params=pltpu.CompilerParams(
            collective_id=0, has_side_effects=True, vmem_limit_bytes=32 * 1024 * 1024
        ),
    )(
        *(
            array if array is tile_count else pltpu.with_memory_space_constraint(array, pltpu.HBM)
            for array in (
                features, w_self, w_neigh, bias.reshape(1, W), cotangent, tile_vals, tile_pos, tile_count,
                by_slot(send_rows), by_slot(recv_dest), by_slot(ghost_weight), recv_count, hub_rows, hub_weight,
            )
        )
    )
    output, grad_features, grad_self, grad_neigh, grad_bias = pl.pallas_call(
        save_kernel,
        out_shape=(
            jax.ShapeDtypeStruct((ROWS, W), BF16),
            jax.ShapeDtypeStruct((ROWS, W), BF16),
            jax.ShapeDtypeStruct((W, cols), F32),
            jax.ShapeDtypeStruct((W, cols), F32),
            jax.ShapeDtypeStruct((1, W), F32),
        ),
        in_specs=[vmem] * 4,
        out_specs=(hbm,) * 5,
        scratch_shapes=[pltpu.SemaphoreType.DMA((3 + 2 * X,))],
    )(*results)
    return output, grad_features, grad_self, grad_neigh, grad_bias.reshape(W)


def solution(mesh):
    placed = (
        P("dom", "feat"),
        P("feat", None),
        P("feat", None),
        P("feat"),
        P("dom", "feat"),
        P("dom", None, None, None),
        P("dom", None),
        P("dom"),
        P("dom", None, None),
        P("dom", None, None),
        P("dom", None, None),
        P("dom", None),
        P("dom", None),
        P("dom", None),
    )
    return jax.shard_map(
        on_device,
        mesh=mesh,
        in_specs=placed,
        out_specs=(P("dom", "feat"), P("dom", "feat"), P("feat", None), P("feat", None), P("feat")),
        check_vma=False,
    )
```

```python
import math

import jax
import jax.numpy as jnp
from jax import lax
from jax.experimental import pallas as pl
from jax.experimental.pallas import tpu as pltpu
from jax.sharding import PartitionSpec as P

Z, Y, CORES, X = 16, 4, 2, 4
YC = Y * CORES
DOM = Z * YC
ROWS, W, TILE = 256, 128, 128
SLOTS, HUB, TMAX = 3, 2, 4
F32, BF16, I32 = jnp.float32, jnp.bfloat16, jnp.int32

ZROWS = 32
B_ROWS = SLOTS * Z + HUB * Z
C_ROWS = B_ROWS + 16
COT_ROWS = ROWS + 16

(ST_A, ST_B, ST_XF, ST_XW, ST_XC, ST_CW, ST_P, ST_C, ST_D, ST_RC, ST_RY, ST_RZ, ST_GZ, ST_GC, ST_GY) = range(15)
STAGES = ST_GY + Y


def iota(shape, axis):
    return lax.broadcasted_iota(I32, shape, axis)


def dot(a, b):
    return jnp.dot(a, b, preferred_element_type=F32)


def dot_t(a, b):
    return lax.dot_general(a, b, (((1,), (1,)), ((), ())), preferred_element_type=F32)


def tdot(a, b):
    return lax.dot_general(a, b, (((0,), (0,)), ((), ())), preferred_element_type=F32)


def onehot(mask):
    return jnp.where(mask, 1.0, 0.0).astype(BF16)


def natural_to_plane():
    n, p = iota((DOM, DOM), 0), iota((DOM, DOM), 1)
    return onehot((n % YC == p // Z) & (n // YC == p % Z))


def hubs_to_plane():
    n, p = iota((DOM * HUB, DOM * HUB), 0), iota((DOM * HUB, DOM * HUB), 1)
    n2, p2 = n // HUB, p // HUB
    return onehot((n % HUB == p % HUB) & (n2 % YC == p2 // Z) & (n2 // YC == p2 % Z))


def hub_pick():
    q, n = iota((HUB * Z, 8 * Z), 0), iota((HUB * Z, 8 * Z), 1)
    return onehot((n // 8 == q // HUB) & (n % 8 == q % HUB))


def kernel(
    feat_h, wself_h, wneigh_h, bias_h, cot_h, tiles_h, pos_h, cnt_s, send_h, dest_h, gw_h, rc_h, hub_h, hw_h,
    out_v, gf_v, wtot, gb_v,
    feat_x, w_x, cot_x, neigh_x, bias_v, tiles, pos_s, send_v, dest_v, gw_v, rc_v, hub_s, hw,
    send_a, recv_a, send_b, recv_b, gp, own_pre, send_c, recv_c, send_d, recv_d,
    g_m, m_m, mt_m, base, pself, wsend, wown, rcore, send_ry, ry, ysum, rz, gz,
    in_sem, send_sem, recv_sem,
):
    d = lax.axis_index("dom")
    f = lax.axis_index("feat")
    z, yc = d // YC, d % YC
    y, c = yc // CORES, yc % CORES
    partner = z * YC + y * CORES + (1 - c)

    def z_peer(k):
        return lax.rem(z + k, Z) * YC + yc

    def plane_peer(k):
        return z * YC + lax.rem(yc + k, YC)

    def y_peer(k):
        return z * YC + lax.rem(y + k, Y) * CORES + c

    def x_peer(k):
        return lax.rem(f + k, X)

    def around(count, step):
        def body(i, carry):
            half = (i + 1) // 2
            step(count // 2 + jnp.where(i % 2 == 1, -half, half))
            return carry

        lax.fori_loop(0, count - 1, body, 0)

    barrier = pltpu.get_barrier_semaphore()

    def greet(dom, feat_at):
        pl.semaphore_signal(barrier, inc=1, device_id=(dom, feat_at), device_id_type=pl.DeviceIdType.MESH)

    around(Z, lambda k: greet(z_peer(k), f))
    around(YC, lambda k: greet(plane_peer(k), f))
    around(X, lambda k: greet(d, x_peer(k)))

    loads = []

    def load(src, dst):
        copy = pltpu.make_async_copy(src, dst, in_sem.at[len(loads)])
        copy.start()
        loads.append(copy)
        return copy

    load_send = load(send_h, send_v)
    load_hub = load(hub_h, hub_s)
    load_feat = load(feat_h, feat_x.at[f])
    load_w = [load(wself_h, w_x.at[0, f]), load(wneigh_h, w_x.at[1, f])]
    load_cot = [load(cot_h, cot_x.at[f, pl.ds(0, ROWS)]), load(bias_h, bias_v)]
    load_edges = [load(dest_h, dest_v), load(gw_h, gw_v), load(rc_h, rc_v)]
    load_tiles = [load(tiles_h, tiles), load(pos_h, pos_s)]
    load_hw = load(hw_h, hw)

    def push(stage, src, dst, dom, feat_at):
        pltpu.make_async_remote_copy(
            src_ref=src,
            dst_ref=dst,
            send_sem=send_sem.at[stage],
            recv_sem=recv_sem.at[stage],
            device_id=(dom, feat_at),
            device_id_type=pl.DeviceIdType.MESH,
        ).start()

    def arrived(stage, ref):
        pltpu.make_async_copy(ref, ref, recv_sem.at[stage]).wait()

    def sent(stage, ref):
        pltpu.make_async_copy(ref, ref, send_sem.at[stage]).wait()

    pending = []

    row_of = iota((ROWS, DOM), 0)
    load_send.wait()
    load_hub.wait()
    for s in range(SLOTS):
        g_m[:, s * DOM : (s + 1) * DOM] = onehot(row_of == send_v[s])
    lane8, sub8 = iota((8, ROWS), 1), iota((8, ROWS), 0)
    own_hub = onehot(((sub8 == 0) & (lane8 == hub_s[0, 0])) | ((sub8 == 1) & (lane8 == hub_s[0, 1])))
    load_feat.wait()
    feat = feat_x[f]
    groups = [tdot(g_m[:, s * DOM : (s + 1) * DOM], feat).reshape(Z, YC, W) for s in range(SLOTS)]
    groups.append(jnp.broadcast_to(dot(own_hub, feat)[None], (Z, 8, W)))
    send_a[...] = jnp.concatenate(groups, axis=1).astype(BF16)

    pl.semaphore_wait(barrier, (Z - 1) + (YC - 1) + (X - 1))
    around(Z, lambda k: push(ST_A, send_a.at[lax.rem(z + k, Z)], recv_a.at[z], z_peer(k), f))
    pending.append((ST_A, send_a.at[pl.ds(0, Z - 1)]))
    recv_a[pl.ds(z, 1)] = send_a[pl.ds(z, 1)]

    around(X, lambda k: push(ST_XF, feat_x.at[f], feat_x.at[f], d, x_peer(k)))
    pending.append((ST_XF, feat_x.at[pl.ds(0, X - 1)]))
    for copy in load_w:
        copy.wait()
    around(X, lambda k: push(ST_XW, w_x.at[c, f], w_x.at[c, f], d, x_peer(k)))
    pending.append((ST_XW, w_x.at[0, pl.ds(0, X - 1)]))
    for copy in load_cot:
        copy.wait()
    bias_rows = jnp.concatenate([bias_v[...].astype(F32), jnp.zeros((15, W), F32)], axis=0)
    cot_x[pl.ds(f, 1), ROWS:] = bias_rows.astype(BF16)[None]
    around(X, lambda k: push(ST_XC, cot_x.at[f], cot_x.at[f], d, x_peer(k)))
    pending.append((ST_XC, cot_x.at[pl.ds(0, X - 1)]))

    to_plane = natural_to_plane()
    pick = hub_pick()
    for copy in load_edges:
        copy.wait()
    live = [jnp.where(rc_v[...] > s, gw_v[s], 0.0) for s in range(SLOTS)]
    packed = jnp.concatenate([dest_v[s].astype(F32) for s in range(SLOTS)] + live + [jnp.zeros((2, DOM), F32)], axis=0)
    packed = dot(packed.astype(BF16), to_plane)
    for s in range(SLOTS):
        dest_row = packed[s : s + 1].astype(I32)
        m_m[:, ROWS + s * DOM : ROWS + (s + 1) * DOM] = jnp.where(
            row_of == dest_row, packed[SLOTS + s : SLOTS + s + 1], 0.0
        ).astype(BF16)

    arrived(ST_A, recv_a.at[pl.ds(0, Z - 1)])
    got = recv_a[...].astype(F32)
    for s in range(SLOTS):
        part = got[:, s * YC : (s + 1) * YC].reshape(DOM, W).astype(BF16)
        send_b[:, s * Z : (s + 1) * Z] = tdot(to_plane, part).reshape(YC, Z, W).astype(BF16)
    hub_rows = dot(pick, got[:, SLOTS * YC :].reshape(Z * 8, W).astype(BF16))
    send_b[:, SLOTS * Z :] = jnp.broadcast_to(hub_rows[None], (YC, HUB * Z, W)).astype(BF16)
    around(YC, lambda k: push(ST_B, send_b.at[lax.rem(yc + k, YC)], recv_b.at[yc], plane_peer(k), f))
    pending.append((ST_B, send_b.at[pl.ds(0, YC - 1)]))
    recv_b[pl.ds(yc, 1)] = send_b[pl.ds(yc, 1)]

    for copy in load_tiles:
        copy.wait()
    tile_f32 = [tiles[0, t].astype(F32) for t in range(TMAX)]
    for k in range(4):
        block = jnp.zeros((TILE, TILE), F32)
        for t in range(TMAX):
            used = jnp.where((pos_s[0, t] == k) & (cnt_s[0] > t), 1.0, 0.0)
            block = block + used * tile_f32[t]
        m_m[(k // 2) * TILE : (k // 2 + 1) * TILE, (k % 2) * TILE : (k % 2 + 1) * TILE] = block.astype(BF16)
    load_hw.wait()
    m_m[:, ROWS + SLOTS * DOM :] = dot(hw[...], hubs_to_plane()).astype(BF16)
    base[...] = dot(m_m[:, :ROWS], feat_x[f])

    arrived(ST_B, recv_b.at[pl.ds(0, YC - 1)])
    pulled = [recv_b[:, s * Z : (s + 1) * Z].reshape(DOM, W) for s in range(SLOTS)]
    pulled.append(recv_b[:, SLOTS * Z :].reshape(DOM * HUB, W))
    neigh = (base[...] + dot(m_m[:, ROWS:], jnp.concatenate(pulled, axis=0))).astype(BF16)
    neigh_x[pl.ds(f, 1)] = neigh[None]
    around(X, lambda k: push(ST_P, neigh_x.at[f], neigh_x.at[f], d, x_peer(k)))
    pending.append((ST_P, neigh_x.at[pl.ds(0, X - 1)]))

    arrived(ST_XW, w_x.at[0, pl.ds(0, X - 1)])
    around(X, lambda k: push(ST_CW, w_x.at[c, x_peer(k)], w_x.at[c, x_peer(k)], partner, f))
    pending.append((ST_CW, w_x.at[0, pl.ds(0, X - 1)]))
    mt_m[...] = m_m[...].T
    arrived(ST_XF, feat_x.at[pl.ds(0, X - 1)])
    arrived(ST_XC, cot_x.at[pl.ds(0, X - 1)])
    arrived(ST_CW, w_x.at[0, pl.ds(0, X - 1)])
    feat_full = jnp.concatenate([feat_x[j] for j in range(X)], axis=1)
    pself[...] = dot(feat_full, w_x[0].reshape(X * W, X * W))

    arrived(ST_P, neigh_x.at[pl.ds(0, X - 1)])
    neigh_full = jnp.concatenate([neigh_x[j] for j in range(X)], axis=1)
    for j in range(X):
        cols = slice(j * W, (j + 1) * W)
        w_cols = jnp.concatenate([w_x[1, i, :, cols] for i in range(X)], axis=0)
        bias_row = cot_x[j, ROWS : ROWS + 16].astype(F32)[0:1]
        preact = pself[:, cols] + dot(neigh_full, w_cols) + bias_row
        own_pre[j] = preact
        logistic = jax.nn.sigmoid(preact)
        gp[j] = (cot_x[j, :ROWS].astype(F32) * logistic * (1.0 + preact * (1.0 - logistic))).astype(BF16)

    first = c == 0
    rows_out = jnp.where(first, neigh_x[f], feat_x[f])
    for j in range(X):
        wsend[j] = tdot(rows_out, gp[j])
    push(ST_RC, wsend, rcore, partner, f)
    pending.append((ST_RC, rcore))
    rows_own = jnp.where(first, feat_x[f], neigh_x[f])
    for j in range(X):
        wown[j] = tdot(rows_own, gp[j])

    gp_full = jnp.concatenate([gp[j] for j in range(X)], axis=1)
    neigh_grad = dot_t(gp_full, w_x[1, f]).astype(BF16)
    back = dot(mt_m[...], neigh_grad)
    for s in range(SLOTS):
        at = ROWS + s * DOM
        send_c[:, s * Z : (s + 1) * Z] = back[at : at + DOM].reshape(YC, Z, W).astype(BF16)
    send_c[:, SLOTS * Z : B_ROWS] = back[ROWS + SLOTS * DOM :].reshape(YC, HUB * Z, W).astype(BF16)

    def two_rows(row, first):
        high = row.astype(BF16).astype(F32)
        at = iota((8, W), 0)
        return jnp.where(at == first, high, jnp.where(at == first + 1, row - high, 0.0))

    bias_part = jnp.sum(gp[f].astype(F32), axis=0, keepdims=True)
    bias_rows = jnp.concatenate([two_rows(bias_part, 0), jnp.zeros((8, W), F32)], axis=0)
    send_c[:, B_ROWS:] = jnp.broadcast_to(bias_rows[None], (YC, 16, W)).astype(BF16)
    around(YC, lambda k: push(ST_C, send_c.at[lax.rem(yc + k, YC)], recv_c.at[yc], plane_peer(k), f))
    pending.append((ST_C, send_c.at[pl.ds(0, YC - 1)]))
    recv_c[pl.ds(yc, 1)] = send_c[pl.ds(yc, 1)]

    arrived(ST_RC, rcore)
    send_ry[...] = (rcore[...] + wown[...]).astype(BF16)
    around(Y, lambda k: push(ST_RY, send_ry.at[lax.rem(y + k, Y)], ry.at[y], y_peer(k), f))
    pending.append((ST_RY, ry.at[pl.ds(0, Y - 1)]))
    ry[pl.ds(y, 1)] = send_ry[pl.ds(y, 1)]
    base[...] = back[:ROWS] + dot_t(gp_full, w_x[0, f])

    arrived(ST_RY, ry.at[pl.ds(0, Y - 1)])
    ysum[...] = jnp.sum(ry[...].astype(F32), axis=0)
    around(
        Z,
        lambda k: push(
            ST_RZ, ysum.at[pl.ds(pl.multiple_of(lax.rem(z + k, Z) * 8, 8), 8)], rz.at[z], z_peer(k), f
        ),
    )
    pending.append((ST_RZ, rz.at[pl.ds(0, Z - 1)]))
    mine = pl.ds(pl.multiple_of(z * 8, 8), 8)
    rz[pl.ds(z, 1)] = ysum[mine][None]

    arrived(ST_C, recv_c.at[pl.ds(0, YC - 1)])
    groups = []
    for s in range(SLOTS):
        part = recv_c[:, s * Z : (s + 1) * Z].reshape(DOM, W)
        groups.append(dot(to_plane, part).reshape(Z, YC, W))
    hub_sum = jnp.sum(recv_c[:, SLOTS * Z : B_ROWS].astype(F32), axis=0)
    bias_sum = jnp.sum(recv_c[:, B_ROWS:].astype(F32), axis=0)
    bias_sum = bias_sum[0:1] + bias_sum[1:2]
    groups.append(tdot(pick, hub_sum.astype(BF16)).reshape(Z, 8, W) + two_rows(bias_sum, HUB)[None])
    send_d[...] = jnp.concatenate(groups, axis=1).astype(BF16)
    around(Z, lambda k: push(ST_D, send_d.at[lax.rem(z + k, Z)], recv_d.at[z], z_peer(k), f))
    pending.append((ST_D, send_d.at[pl.ds(0, Z - 1)]))
    recv_d[pl.ds(z, 1)] = send_d[pl.ds(z, 1)]
    preact = own_pre[f]
    out_v[...] = (preact * jax.nn.sigmoid(preact)).astype(BF16)

    arrived(ST_RZ, rz.at[pl.ds(0, Z - 1)])
    scale = 1.0 / math.sqrt(DOM * ROWS)
    gz[mine] = jnp.sum(rz[...], axis=0) * scale
    around(Z, lambda k: push(ST_GZ, gz.at[mine], gz.at[mine], z_peer(k), f))
    pending.append((ST_GZ, rz.at[pl.ds(0, Z - 1)]))

    arrived(ST_D, recv_d.at[pl.ds(0, Z - 1)])
    got = recv_d[...].astype(F32)
    pieces = [got[:, s * YC : (s + 1) * YC].reshape(DOM, W).astype(BF16) for s in range(SLOTS)]
    total = base[...] + dot(g_m[...], jnp.concatenate(pieces, axis=0))
    last = jnp.sum(got[:, SLOTS * YC :], axis=0)
    at_row = iota((ROWS, W), 0)
    for k in range(HUB):
        total = total + jnp.where(at_row == hub_s[0, k], last[k : k + 1], 0.0)
    gf_v[...] = total.astype(BF16)
    gb_v[...] = (last[HUB : HUB + 1] + last[HUB + 1 : HUB + 2]) * scale

    arrived(ST_GZ, gz.at[pl.ds(0, (Z - 1) * 8)])
    wtot[c, y] = gz[...].astype(BF16)
    for k in (2, 1, 3):
        push(ST_GY + k, wtot.at[c, y], wtot.at[c, y], y_peer(k), f)
        pending.append((ST_GY + k, wtot.at[0, 0]))
    push(ST_GC, wtot.at[c, y], wtot.at[c, y], partner, f)
    for k in (1, 3, 2):
        source = lax.rem(y + Y - k, Y)
        arrived(ST_GY + k, wtot.at[c, source])
        push(ST_GC, wtot.at[c, source], wtot.at[c, source], partner, f)
    pending.append((ST_GC, wtot.at[0]))
    arrived(ST_GC, wtot.at[1 - c])
    for stage, ref in pending:
        sent(stage, ref)


def save_kernel(out_v, gf_v, wtot, gb_v, out_h, gf_h, gs_h, gn_h, gb_h, gs_v, gn_v, sem):
    copies = []

    def save(src, dst):
        copies.append(pltpu.make_async_copy(src, dst, sem.at[len(copies)]))
        copies[-1].start()

    save(out_v, out_h)
    save(gf_v, gf_h)
    save(gb_v, gb_h)
    for i, (wide, target) in enumerate(((gs_v, gs_h), (gn_v, gn_h))):
        for j in range(X):
            wide[:, j * W : (j + 1) * W] = wtot[i, j].astype(F32)
        save(wide, target)
    for copy in copies:
        copy.wait()


def on_device(
    features, w_self, w_neigh, bias, cotangent, tile_vals, tile_pos, tile_count,
    send_rows, recv_dest, ghost_weight, recv_count, hub_rows, hub_weight,
):
    def by_slot(array):
        return jnp.transpose(array, (2, 0, 1))

    hbm = pl.BlockSpec(memory_space=pltpu.HBM)
    vmem = pl.BlockSpec(memory_space=pltpu.VMEM)
    smem = pl.BlockSpec(memory_space=pltpu.SMEM)
    cols = X * W
    rest = SLOTS * DOM + HUB * DOM
    results = pl.pallas_call(
        kernel,
        out_shape=(
            pltpu.VMEM((ROWS, W), BF16),
            pltpu.VMEM((ROWS, W), BF16),
            pltpu.VMEM((2, Y, W, W), BF16),
            pltpu.VMEM((1, W), F32),
        ),
        in_specs=[hbm] * 7 + [smem] + [hbm] * 6,
        out_specs=(vmem,) * 4,
        scratch_shapes=[
            pltpu.VMEM((X, ROWS, W), BF16),
            pltpu.VMEM((2, X, W, cols), BF16),
            pltpu.VMEM((X, COT_ROWS, W), BF16),
            pltpu.VMEM((X, ROWS, W), BF16),
            pltpu.VMEM((1, W), BF16),
            pltpu.VMEM((1, TMAX, TILE, TILE), BF16),
            pltpu.SMEM((1, TMAX), I32),
            pltpu.VMEM((SLOTS, 1, DOM), I32),
            pltpu.VMEM((SLOTS, 1, DOM), I32),
            pltpu.VMEM((SLOTS, 1, DOM), F32),
            pltpu.VMEM((1, DOM), I32),
            pltpu.SMEM((1, HUB), I32),
            pltpu.VMEM((ROWS, HUB * DOM), BF16),
            pltpu.VMEM((Z, ZROWS, W), BF16),
            pltpu.VMEM((Z, ZROWS, W), BF16),
            pltpu.VMEM((YC, B_ROWS, W), BF16),
            pltpu.VMEM((YC, B_ROWS, W), BF16),
            pltpu.VMEM((X, ROWS, W), BF16),
            pltpu.VMEM((X, ROWS, W), F32),
            pltpu.VMEM((YC, C_ROWS, W), BF16),
            pltpu.VMEM((YC, C_ROWS, W), BF16),
            pltpu.VMEM((Z, ZROWS, W), BF16),
            pltpu.VMEM((Z, ZROWS, W), BF16),
            pltpu.VMEM((ROWS, SLOTS * DOM), BF16),
            pltpu.VMEM((ROWS, ROWS + rest), BF16),
            pltpu.VMEM((ROWS + rest, ROWS), BF16),
            pltpu.VMEM((ROWS, W), F32),
            pltpu.VMEM((ROWS, cols), F32),
            pltpu.VMEM((Y, W, W), F32),
            pltpu.VMEM((Y, W, W), F32),
            pltpu.VMEM((Y, W, W), F32),
            pltpu.VMEM((Y, W, W), BF16),
            pltpu.VMEM((Y, W, W), BF16),
            pltpu.VMEM((W, W), F32),
            pltpu.VMEM((Z, 8, W), F32),
            pltpu.VMEM((W, W), F32),
            pltpu.SemaphoreType.DMA((13,)),
            pltpu.SemaphoreType.DMA((STAGES,)),
            pltpu.SemaphoreType.DMA((STAGES,)),
        ],
        compiler_params=pltpu.CompilerParams(
            collective_id=0, has_side_effects=True, vmem_limit_bytes=32 * 1024 * 1024
        ),
    )(
        *(
            array if array is tile_count else pltpu.with_memory_space_constraint(array, pltpu.HBM)
            for array in (
                features, w_self, w_neigh, bias.reshape(1, W), cotangent, tile_vals, tile_pos, tile_count,
                by_slot(send_rows), by_slot(recv_dest), by_slot(ghost_weight), recv_count, hub_rows, hub_weight,
            )
        )
    )
    output, grad_features, grad_self, grad_neigh, grad_bias = pl.pallas_call(
        save_kernel,
        out_shape=(
            jax.ShapeDtypeStruct((ROWS, W), BF16),
            jax.ShapeDtypeStruct((ROWS, W), BF16),
            jax.ShapeDtypeStruct((W, cols), F32),
            jax.ShapeDtypeStruct((W, cols), F32),
            jax.ShapeDtypeStruct((1, W), F32),
        ),
        in_specs=[vmem] * 4,
        out_specs=(hbm,) * 5,
        scratch_shapes=[
            pltpu.VMEM((W, cols), F32),
            pltpu.VMEM((W, cols), F32),
            pltpu.SemaphoreType.DMA((5,)),
        ],
    )(*(pltpu.with_memory_space_constraint(array, pltpu.VMEM) for array in results))
    return output, grad_features, grad_self, grad_neigh, grad_bias.reshape(W)


def solution(mesh):
    placed = (
        P("dom", "feat"),
        P("feat", None),
        P("feat", None),
        P("feat"),
        P("dom", "feat"),
        P("dom", None, None, None),
        P("dom", None),
        P("dom"),
        P("dom", None, None),
        P("dom", None, None),
        P("dom", None, None),
        P("dom", None),
        P("dom", None),
        P("dom", None),
    )
    return jax.shard_map(
        on_device,
        mesh=mesh,
        in_specs=placed,
        out_specs=(P("dom", "feat"), P("dom", "feat"), P("feat", None), P("feat", None), P("feat")),
        check_vma=False,
    )
```

```python
import math

import jax
import jax.numpy as jnp
from jax import lax
from jax.experimental import pallas as pl
from jax.experimental.pallas import tpu as pltpu
from jax.sharding import PartitionSpec as P

Z, Y, CORES, X = 16, 4, 2, 4
YC = Y * CORES
DOM = Z * YC
ROWS, W, TILE = 256, 128, 128
SLOTS, HUB, TMAX = 3, 2, 4
F32, BF16, I32 = jnp.float32, jnp.bfloat16, jnp.int32

ZROWS = 32
B_ROWS = SLOTS * Z + HUB * Z
C_ROWS = B_ROWS + 16
COT_ROWS = ROWS + 16
WROWS = W // Y
OWNERS = 8
GROWS = W // OWNERS

(ST_A, ST_B, ST_XF, ST_XW, ST_XC, ST_CW, ST_P, ST_C, ST_D, ST_RC, ST_RY, ST_RZ, ST_GZ, ST_GC, ST_YW, ST_GY) = range(16)
STAGES = ST_GY + Y


def iota(shape, axis):
    return lax.broadcasted_iota(I32, shape, axis)


def dot(a, b):
    return jnp.dot(a, b, preferred_element_type=F32)


def dot_t(a, b):
    return lax.dot_general(a, b, (((1,), (1,)), ((), ())), preferred_element_type=F32)


def tdot(a, b):
    return lax.dot_general(a, b, (((0,), (0,)), ((), ())), preferred_element_type=F32)


def onehot(mask):
    return jnp.where(mask, 1.0, 0.0).astype(BF16)


def natural_to_plane():
    n, p = iota((DOM, DOM), 0), iota((DOM, DOM), 1)
    return onehot((n % YC == p // Z) & (n // YC == p % Z))


def hubs_to_plane():
    n, p = iota((DOM * HUB, DOM * HUB), 0), iota((DOM * HUB, DOM * HUB), 1)
    n2, p2 = n // HUB, p // HUB
    return onehot((n % HUB == p % HUB) & (n2 % YC == p2 // Z) & (n2 // YC == p2 % Z))


def hub_pick():
    q, n = iota((HUB * Z, 8 * Z), 0), iota((HUB * Z, 8 * Z), 1)
    return onehot((n // 8 == q // HUB) & (n % 8 == q % HUB))


def kernel(
    feat_h, wself_h, wneigh_h, bias_h, cot_h, tiles_h, pos_h, cnt_s, send_h, dest_h, gw_h, rc_h, hub_h, hw_h,
    out_v, gf_v, wtot, gb_v,
    feat_x, w_x, cot_x, neigh_x, bias_v, tiles, pos_s, send_v, dest_v, gw_v, rc_v, hub_s, hw,
    send_a, recv_a, send_b, recv_b, gp, own_pre, send_c, recv_c, send_d, recv_d,
    g_m, m_m, mt_m, base, pself, wsend, wown, rcore, send_ry, ry, ysum, rz,
    in_sem, send_sem, recv_sem,
):
    d = lax.axis_index("dom")
    f = lax.axis_index("feat")
    z, yc = d // YC, d % YC
    y, c = yc // CORES, yc % CORES
    partner = z * YC + y * CORES + (1 - c)

    def z_peer(k):
        return lax.rem(z + k, Z) * YC + yc

    def plane_peer(k):
        return z * YC + lax.rem(yc + k, YC)

    def y_peer(k):
        return z * YC + lax.rem(y + k, Y) * CORES + c

    def x_peer(k):
        return lax.rem(f + k, X)

    def around(count, step):
        def body(i, carry):
            half = (i + 1) // 2
            step(count // 2 + jnp.where(i % 2 == 1, -half, half))
            return carry

        lax.fori_loop(0, count - 1, body, 0)

    barrier = pltpu.get_barrier_semaphore()

    def greet(dom, feat_at):
        pl.semaphore_signal(barrier, inc=1, device_id=(dom, feat_at), device_id_type=pl.DeviceIdType.MESH)

    around(Z, lambda k: greet(z_peer(k), f))
    around(YC, lambda k: greet(plane_peer(k), f))
    around(X, lambda k: greet(d, x_peer(k)))

    loads = []

    def load(src, dst):
        copy = pltpu.make_async_copy(src, dst, in_sem.at[len(loads)])
        copy.start()
        loads.append(copy)
        return copy

    load_send = load(send_h, send_v)
    load_hub = load(hub_h, hub_s)
    load_feat = load(feat_h, feat_x.at[f])
    load_w = [load(wself_h, w_x.at[0, f]), load(wneigh_h, w_x.at[1, f])]
    load_cot = [load(cot_h, cot_x.at[f, pl.ds(0, ROWS)]), load(bias_h, bias_v)]
    load_edges = [load(dest_h, dest_v), load(gw_h, gw_v), load(rc_h, rc_v)]
    load_tiles = [load(tiles_h, tiles), load(pos_h, pos_s)]
    load_hw = load(hw_h, hw)

    def push(stage, src, dst, dom, feat_at):
        pltpu.make_async_remote_copy(
            src_ref=src,
            dst_ref=dst,
            send_sem=send_sem.at[stage],
            recv_sem=recv_sem.at[stage],
            device_id=(dom, feat_at),
            device_id_type=pl.DeviceIdType.MESH,
        ).start()

    def arrived(stage, ref):
        pltpu.make_async_copy(ref, ref, recv_sem.at[stage]).wait()

    def sent(stage, ref):
        pltpu.make_async_copy(ref, ref, send_sem.at[stage]).wait()

    pending = []

    row_of = iota((ROWS, DOM), 0)
    load_send.wait()
    load_hub.wait()
    for s in range(SLOTS):
        g_m[:, s * DOM : (s + 1) * DOM] = onehot(row_of == send_v[s])
    lane8, sub8 = iota((8, ROWS), 1), iota((8, ROWS), 0)
    own_hub = onehot(((sub8 == 0) & (lane8 == hub_s[0, 0])) | ((sub8 == 1) & (lane8 == hub_s[0, 1])))
    load_feat.wait()
    feat = feat_x[f]
    groups = [tdot(g_m[:, s * DOM : (s + 1) * DOM], feat).reshape(Z, YC, W) for s in range(SLOTS)]
    groups.append(jnp.broadcast_to(dot(own_hub, feat)[None], (Z, 8, W)))
    send_a[...] = jnp.concatenate(groups, axis=1).astype(BF16)

    pl.semaphore_wait(barrier, (Z - 1) + (YC - 1) + (X - 1))
    around(Z, lambda k: push(ST_A, send_a.at[lax.rem(z + k, Z)], recv_a.at[z], z_peer(k), f))
    pending.append((ST_A, send_a.at[pl.ds(0, Z - 1)]))
    recv_a[pl.ds(z, 1)] = send_a[pl.ds(z, 1)]

    quarter = pl.ds(pl.multiple_of(y * WROWS, WROWS), WROWS)
    for copy in load_w:
        copy.wait()
    around(X, lambda k: push(ST_XW, w_x.at[c, f, quarter], w_x.at[c, f, quarter], d, x_peer(k)))
    pending.append((ST_XW, w_x.at[0, 0, pl.ds(0, (X - 1) * WROWS)]))
    around(X, lambda k: push(ST_XF, feat_x.at[f], feat_x.at[f], d, x_peer(k)))
    pending.append((ST_XF, feat_x.at[pl.ds(0, X - 1)]))
    for copy in load_cot:
        copy.wait()
    bias_rows = jnp.concatenate([bias_v[...].astype(F32), jnp.zeros((15, W), F32)], axis=0)
    cot_x[pl.ds(f, 1), ROWS:] = bias_rows.astype(BF16)[None]
    around(X, lambda k: push(ST_XC, cot_x.at[f], cot_x.at[f], d, x_peer(k)))
    pending.append((ST_XC, cot_x.at[pl.ds(0, X - 1)]))

    to_plane = natural_to_plane()
    pick = hub_pick()
    for copy in load_edges:
        copy.wait()
    live = [jnp.where(rc_v[...] > s, gw_v[s], 0.0) for s in range(SLOTS)]
    packed = jnp.concatenate([dest_v[s].astype(F32) for s in range(SLOTS)] + live + [jnp.zeros((2, DOM), F32)], axis=0)
    packed = dot(packed.astype(BF16), to_plane)
    for s in range(SLOTS):
        dest_row = packed[s : s + 1].astype(I32)
        m_m[:, ROWS + s * DOM : ROWS + (s + 1) * DOM] = jnp.where(
            row_of == dest_row, packed[SLOTS + s : SLOTS + s + 1], 0.0
        ).astype(BF16)

    arrived(ST_XW, w_x.at[0, 0, pl.ds(0, (X - 1) * WROWS)])

    def weight_on(j):
        shard = w_x.at[c, x_peer(j), quarter]
        around(Y, lambda k: push(ST_YW, shard, shard, y_peer(k), f))

    around(X, weight_on)
    pending.append((ST_YW, w_x.at[0, pl.ds(0, X - 1), pl.ds(0, (Y - 1) * WROWS)]))

    arrived(ST_A, recv_a.at[pl.ds(0, Z - 1)])
    got = recv_a[...].astype(F32)
    for s in range(SLOTS):
        part = got[:, s * YC : (s + 1) * YC].reshape(DOM, W).astype(BF16)
        send_b[:, s * Z : (s + 1) * Z] = tdot(to_plane, part).reshape(YC, Z, W).astype(BF16)
    hub_rows = dot(pick, got[:, SLOTS * YC :].reshape(Z * 8, W).astype(BF16))
    send_b[:, SLOTS * Z :] = jnp.broadcast_to(hub_rows[None], (YC, HUB * Z, W)).astype(BF16)
    around(YC, lambda k: push(ST_B, send_b.at[lax.rem(yc + k, YC)], recv_b.at[yc], plane_peer(k), f))
    pending.append((ST_B, send_b.at[pl.ds(0, YC - 1)]))
    recv_b[pl.ds(yc, 1)] = send_b[pl.ds(yc, 1)]

    for copy in load_tiles:
        copy.wait()
    tile_f32 = [tiles[0, t].astype(F32) for t in range(TMAX)]
    for k in range(4):
        block = jnp.zeros((TILE, TILE), F32)
        for t in range(TMAX):
            used = jnp.where((pos_s[0, t] == k) & (cnt_s[0] > t), 1.0, 0.0)
            block = block + used * tile_f32[t]
        m_m[(k // 2) * TILE : (k // 2 + 1) * TILE, (k % 2) * TILE : (k % 2 + 1) * TILE] = block.astype(BF16)
    load_hw.wait()
    m_m[:, ROWS + SLOTS * DOM :] = dot(hw[...], hubs_to_plane()).astype(BF16)
    base[...] = dot(m_m[:, :ROWS], feat_x[f])

    arrived(ST_B, recv_b.at[pl.ds(0, YC - 1)])
    pulled = [recv_b[:, s * Z : (s + 1) * Z].reshape(DOM, W) for s in range(SLOTS)]
    pulled.append(recv_b[:, SLOTS * Z :].reshape(DOM * HUB, W))
    neigh = (base[...] + dot(m_m[:, ROWS:], jnp.concatenate(pulled, axis=0))).astype(BF16)
    neigh_x[pl.ds(f, 1)] = neigh[None]
    around(X, lambda k: push(ST_P, neigh_x.at[f], neigh_x.at[f], d, x_peer(k)))
    pending.append((ST_P, neigh_x.at[pl.ds(0, X - 1)]))

    arrived(ST_YW, w_x.at[0, pl.ds(0, X - 1), pl.ds(0, (Y - 1) * WROWS)])
    around(X, lambda k: push(ST_CW, w_x.at[c, x_peer(k)], w_x.at[c, x_peer(k)], partner, f))
    pending.append((ST_CW, w_x.at[0, pl.ds(0, X - 1)]))
    mt_m[...] = m_m[...].T
    arrived(ST_XF, feat_x.at[pl.ds(0, X - 1)])
    arrived(ST_XC, cot_x.at[pl.ds(0, X - 1)])
    arrived(ST_CW, w_x.at[0, pl.ds(0, X - 1)])
    feat_full = jnp.concatenate([feat_x[j] for j in range(X)], axis=1)
    pself[...] = dot(feat_full, w_x[0].reshape(X * W, X * W))

    arrived(ST_P, neigh_x.at[pl.ds(0, X - 1)])
    neigh_full = jnp.concatenate([neigh_x[j] for j in range(X)], axis=1)
    for j in range(X):
        cols = slice(j * W, (j + 1) * W)
        w_cols = jnp.concatenate([w_x[1, i, :, cols] for i in range(X)], axis=0)
        bias_row = cot_x[j, ROWS : ROWS + 16].astype(F32)[0:1]
        preact = pself[:, cols] + dot(neigh_full, w_cols) + bias_row
        own_pre[j] = preact
        logistic = jax.nn.sigmoid(preact)
        gp[j] = (cot_x[j, :ROWS].astype(F32) * logistic * (1.0 + preact * (1.0 - logistic))).astype(BF16)

    first = c == 0
    rows_out = jnp.where(first, neigh_x[f], feat_x[f])
    for j in range(X):
        wsend[j] = tdot(rows_out, gp[j])
    push(ST_RC, wsend, rcore, partner, f)
    pending.append((ST_RC, rcore))
    rows_own = jnp.where(first, feat_x[f], neigh_x[f])
    for j in range(X):
        wown[j] = tdot(rows_own, gp[j])

    arrived(ST_RC, rcore)
    send_ry[...] = (rcore[...] + wown[...]).astype(BF16)
    around(Y, lambda k: push(ST_RY, send_ry.at[lax.rem(y + k, Y)], ry.at[y], y_peer(k), f))
    pending.append((ST_RY, ry.at[pl.ds(0, Y - 1)]))
    ry[pl.ds(y, 1)] = send_ry[pl.ds(y, 1)]

    gp_full = jnp.concatenate([gp[j] for j in range(X)], axis=1)
    neigh_grad = dot_t(gp_full, w_x[1, f]).astype(BF16)
    back = dot(mt_m[...], neigh_grad)
    for s in range(SLOTS):
        at = ROWS + s * DOM
        send_c[:, s * Z : (s + 1) * Z] = back[at : at + DOM].reshape(YC, Z, W).astype(BF16)
    send_c[:, SLOTS * Z : B_ROWS] = back[ROWS + SLOTS * DOM :].reshape(YC, HUB * Z, W).astype(BF16)

    def two_rows(row, first):
        high = row.astype(BF16).astype(F32)
        at = iota((8, W), 0)
        return jnp.where(at == first, high, jnp.where(at == first + 1, row - high, 0.0))

    bias_part = jnp.sum(gp[f].astype(F32), axis=0, keepdims=True)
    bias_rows = jnp.concatenate([two_rows(bias_part, 0), jnp.zeros((8, W), F32)], axis=0)
    send_c[:, B_ROWS:] = jnp.broadcast_to(bias_rows[None], (YC, 16, W)).astype(BF16)
    around(YC, lambda k: push(ST_C, send_c.at[lax.rem(yc + k, YC)], recv_c.at[yc], plane_peer(k), f))
    pending.append((ST_C, send_c.at[pl.ds(0, YC - 1)]))
    recv_c[pl.ds(yc, 1)] = send_c[pl.ds(yc, 1)]

    base[...] = back[:ROWS] + dot_t(gp_full, w_x[0, f])

    arrived(ST_RY, ry.at[pl.ds(0, Y - 1)])
    ysum[...] = jnp.sum(ry[...].astype(F32), axis=0).astype(BF16)

    def chunk(owner):
        return pl.ds(pl.multiple_of(lax.rem(owner, OWNERS) * GROWS, GROWS), GROWS)

    around(Z, lambda k: push(ST_RZ, ysum.at[chunk(z + k)], rz.at[z], z_peer(k), f))
    pending.append((ST_RZ, rz.at[pl.ds(0, Z - 1)]))
    mine = chunk(z)
    rz[pl.ds(z, 1)] = ysum[mine][None]
    preact = own_pre[f]
    out_v[...] = (preact * jax.nn.sigmoid(preact)).astype(BF16)

    arrived(ST_C, recv_c.at[pl.ds(0, YC - 1)])
    groups = []
    for s in range(SLOTS):
        part = recv_c[:, s * Z : (s + 1) * Z].reshape(DOM, W)
        groups.append(dot(to_plane, part).reshape(Z, YC, W))
    hub_sum = jnp.sum(recv_c[:, SLOTS * Z : B_ROWS].astype(F32), axis=0)
    bias_sum = jnp.sum(recv_c[:, B_ROWS:].astype(F32), axis=0)
    bias_sum = bias_sum[0:1] + bias_sum[1:2]
    groups.append(tdot(pick, hub_sum.astype(BF16)).reshape(Z, 8, W) + two_rows(bias_sum, HUB)[None])
    send_d[...] = jnp.concatenate(groups, axis=1).astype(BF16)

    arrived(ST_RZ, rz.at[pl.ds(0, Z - 1)])
    scale = 1.0 / math.sqrt(DOM * ROWS)
    wtot[c, y, mine] = (jnp.sum(rz[...].astype(F32), axis=0) * scale).astype(BF16)

    def near(k):
        return z_peer(jnp.where(k > OWNERS // 2, k + Z - OWNERS, k))

    around(OWNERS, lambda k: push(ST_GZ, wtot.at[c, y, mine], wtot.at[c, y, mine], near(k), f))
    pending.append((ST_GZ, rz.at[pl.ds(0, OWNERS - 1)]))
    around(Z, lambda k: push(ST_D, send_d.at[lax.rem(z + k, Z)], recv_d.at[z], z_peer(k), f))
    pending.append((ST_D, send_d.at[pl.ds(0, Z - 1)]))
    recv_d[pl.ds(z, 1)] = send_d[pl.ds(z, 1)]

    arrived(ST_GZ, rz.at[pl.ds(0, OWNERS - 1)])
    for k in (2, 1, 3):
        push(ST_GY + k, wtot.at[c, y], wtot.at[c, y], y_peer(k), f)
        pending.append((ST_GY + k, wtot.at[0, 0]))
    push(ST_GC, wtot.at[c, y], wtot.at[c, y], partner, f)
    for k in (1, 3, 2):
        source = lax.rem(y + Y - k, Y)
        arrived(ST_GY + k, wtot.at[c, source])
        push(ST_GC, wtot.at[c, source], wtot.at[c, source], partner, f)
    pending.append((ST_GC, wtot.at[0]))

    arrived(ST_D, recv_d.at[pl.ds(0, Z - 1)])
    got = recv_d[...].astype(F32)
    pieces = [got[:, s * YC : (s + 1) * YC].reshape(DOM, W).astype(BF16) for s in range(SLOTS)]
    total = base[...] + dot(g_m[...], jnp.concatenate(pieces, axis=0))
    last = jnp.sum(got[:, SLOTS * YC :], axis=0)
    at_row = iota((ROWS, W), 0)
    for k in range(HUB):
        total = total + jnp.where(at_row == hub_s[0, k], last[k : k + 1], 0.0)
    gf_v[...] = total.astype(BF16)
    gb_v[...] = (last[HUB : HUB + 1] + last[HUB + 1 : HUB + 2]) * scale

    arrived(ST_GC, wtot.at[1 - c])
    for stage, ref in pending:
        sent(stage, ref)


def save_kernel(out_v, gf_v, wtot, gb_v, out_h, gf_h, gs_h, gn_h, gb_h, gs_v, gn_v, sem):
    copies = []

    def save(src, dst):
        copies.append(pltpu.make_async_copy(src, dst, sem.at[len(copies)]))
        copies[-1].start()

    save(out_v, out_h)
    save(gf_v, gf_h)
    save(gb_v, gb_h)
    for i, (wide, target) in enumerate(((gs_v, gs_h), (gn_v, gn_h))):
        for j in range(X):
            wide[:, j * W : (j + 1) * W] = wtot[i, j].astype(F32)
        save(wide, target)
    for copy in copies:
        copy.wait()


def on_device(
    features, w_self, w_neigh, bias, cotangent, tile_vals, tile_pos, tile_count,
    send_rows, recv_dest, ghost_weight, recv_count, hub_rows, hub_weight,
):
    def by_slot(array):
        return jnp.transpose(array, (2, 0, 1))

    hbm = pl.BlockSpec(memory_space=pltpu.HBM)
    vmem = pl.BlockSpec(memory_space=pltpu.VMEM)
    smem = pl.BlockSpec(memory_space=pltpu.SMEM)
    cols = X * W
    rest = SLOTS * DOM + HUB * DOM
    results = pl.pallas_call(
        kernel,
        out_shape=(
            pltpu.VMEM((ROWS, W), BF16),
            pltpu.VMEM((ROWS, W), BF16),
            pltpu.VMEM((2, Y, W, W), BF16),
            pltpu.VMEM((1, W), F32),
        ),
        in_specs=[hbm] * 7 + [smem] + [hbm] * 6,
        out_specs=(vmem,) * 4,
        scratch_shapes=[
            pltpu.VMEM((X, ROWS, W), BF16),
            pltpu.VMEM((2, X, W, cols), BF16),
            pltpu.VMEM((X, COT_ROWS, W), BF16),
            pltpu.VMEM((X, ROWS, W), BF16),
            pltpu.VMEM((1, W), BF16),
            pltpu.VMEM((1, TMAX, TILE, TILE), BF16),
            pltpu.SMEM((1, TMAX), I32),
            pltpu.VMEM((SLOTS, 1, DOM), I32),
            pltpu.VMEM((SLOTS, 1, DOM), I32),
            pltpu.VMEM((SLOTS, 1, DOM), F32),
            pltpu.VMEM((1, DOM), I32),
            pltpu.SMEM((1, HUB), I32),
            pltpu.VMEM((ROWS, HUB * DOM), BF16),
            pltpu.VMEM((Z, ZROWS, W), BF16),
            pltpu.VMEM((Z, ZROWS, W), BF16),
            pltpu.VMEM((YC, B_ROWS, W), BF16),
            pltpu.VMEM((YC, B_ROWS, W), BF16),
            pltpu.VMEM((X, ROWS, W), BF16),
            pltpu.VMEM((X, ROWS, W), F32),
            pltpu.VMEM((YC, C_ROWS, W), BF16),
            pltpu.VMEM((YC, C_ROWS, W), BF16),
            pltpu.VMEM((Z, ZROWS, W), BF16),
            pltpu.VMEM((Z, ZROWS, W), BF16),
            pltpu.VMEM((ROWS, SLOTS * DOM), BF16),
            pltpu.VMEM((ROWS, ROWS + rest), BF16),
            pltpu.VMEM((ROWS + rest, ROWS), BF16),
            pltpu.VMEM((ROWS, W), F32),
            pltpu.VMEM((ROWS, cols), F32),
            pltpu.VMEM((Y, W, W), F32),
            pltpu.VMEM((Y, W, W), F32),
            pltpu.VMEM((Y, W, W), F32),
            pltpu.VMEM((Y, W, W), BF16),
            pltpu.VMEM((Y, W, W), BF16),
            pltpu.VMEM((W, W), BF16),
            pltpu.VMEM((Z, GROWS, W), BF16),
            pltpu.SemaphoreType.DMA((13,)),
            pltpu.SemaphoreType.DMA((STAGES,)),
            pltpu.SemaphoreType.DMA((STAGES,)),
        ],
        compiler_params=pltpu.CompilerParams(
            collective_id=0, has_side_effects=True, vmem_limit_bytes=32 * 1024 * 1024
        ),
    )(
        *(
            array if array is tile_count else pltpu.with_memory_space_constraint(array, pltpu.HBM)
            for array in (
                features, w_self, w_neigh, bias.reshape(1, W), cotangent, tile_vals, tile_pos, tile_count,
                by_slot(send_rows), by_slot(recv_dest), by_slot(ghost_weight), recv_count, hub_rows, hub_weight,
            )
        )
    )
    output, grad_features, grad_self, grad_neigh, grad_bias = pl.pallas_call(
        save_kernel,
        out_shape=(
            jax.ShapeDtypeStruct((ROWS, W), BF16),
            jax.ShapeDtypeStruct((ROWS, W), BF16),
            jax.ShapeDtypeStruct((W, cols), F32),
            jax.ShapeDtypeStruct((W, cols), F32),
            jax.ShapeDtypeStruct((1, W), F32),
        ),
        in_specs=[vmem] * 4,
        out_specs=(hbm,) * 5,
        scratch_shapes=[
            pltpu.VMEM((W, cols), F32),
            pltpu.VMEM((W, cols), F32),
            pltpu.SemaphoreType.DMA((5,)),
        ],
    )(*(pltpu.with_memory_space_constraint(array, pltpu.VMEM) for array in results))
    return output, grad_features, grad_self, grad_neigh, grad_bias.reshape(W)


def solution(mesh):
    placed = (
        P("dom", "feat"),
        P("feat", None),
        P("feat", None),
        P("feat"),
        P("dom", "feat"),
        P("dom", None, None, None),
        P("dom", None),
        P("dom"),
        P("dom", None, None),
        P("dom", None, None),
        P("dom", None, None),
        P("dom", None),
        P("dom", None),
        P("dom", None),
    )
    return jax.shard_map(
        on_device,
        mesh=mesh,
        in_specs=placed,
        out_specs=(P("dom", "feat"), P("dom", "feat"), P("feat", None), P("feat", None), P("feat")),
        check_vma=False,
    )
```
